32 devices in a mesh: section: 4 (over z), rows: 8 (over y, x, core).
Axes of the slice: x: 2, y: 2, z: 4, core: 2. Of those that a mesh axis runs over, the one named last changes fastest.
Arguments:
- latents: bfloat16 [4, 2, 8, 48, 384], P('section', None, 'rows'), may hold values from -6 to 6
- conv_weight: bfloat16 [4, 3, 3, 3, 384, 384], P('section'), may hold values from -0.0625 to 0.0625
- gain: float32 [4, 384], P('section'), may hold values from 0.5 to 2
- bias: float32 [4, 384], P('section'), may hold values from -0.5 to 0.5
Outputs:
- decoded: bfloat16 [4, 2, 8, 48, 384], P('section', None, 'rows')
The draws below stay inside these ranges and needn't reach their ends.
All inputs are finite; a program needn't handle non-finite values.
Results may differ from the reference program's by a relative error of at most 0.017.
Values may be sent and summed in bfloat16 or wider, within the bound.
A program may use at most 64 MiB of HBM per device.

```python
import math
import jax
import jax.numpy as jnp
from jax import lax

C = 384
F = 2
W = 48
SECTIONS = 4
BLOCKS = 4
H = 8


def block_scale(key, extent, cuts, low, largest):
    def one(axis_at, blocks):
        heights = jax.random.uniform(jax.random.fold_in(jax.random.fold_in(key, 6), axis_at), (blocks,), jnp.float32, low / len(cuts), largest / len(cuts))
        return jnp.repeat(jnp.exp(heights), extent[axis_at] // blocks).reshape((-1,) + (1,) * (len(extent) - axis_at - 1))

    level = one(*cuts[0])
    for cut in cuts[1:]:
        level = level * one(*cut)
    return level


def noise(key, shape, scale, reach, shards=(), dtype=jnp.bfloat16):
    level = block_scale(key, shape, shards, -0.22, 0.18) if shards else 1.0
    values = jax.random.normal(key, shape, jnp.float32) * scale * level
    return jnp.minimum(jnp.maximum(values, -reach), reach).astype(dtype)


def setup_inputs(seed: int = 0) -> dict:
    streams_of = jax.random.split(jax.random.key(seed), 5)
    latents = noise(streams_of[0], (BLOCKS, F, H, W, C), 1.0, 6.0, ((0, 4), (2, 8)))
    conv_weight = noise(streams_of[1], (SECTIONS, 3, 3, 3, C, C), (27 * C) ** -0.5, 0.0625, ((0, 4),))
    gain = jnp.clip(jnp.exp(math.log(2.0) - 1.3862944 * jax.random.uniform(streams_of[2], (SECTIONS, C), jnp.float32) ** block_scale(streams_of[2], (SECTIONS, C), ((0, 4),), -0.2, 0.2)), 0.5, 2.0)
    bias = jnp.clip(jax.random.uniform(streams_of[3], (SECTIONS, C), jnp.float32, -0.5, 0.5) * block_scale(streams_of[3], (SECTIONS, C), ((0, 4),), -0.4, 0.0), -0.5, 0.5)
    return {"latents": latents, "conv_weight": conv_weight, "gain": gain, "bias": bias}


epsilon = 1e-06

def normed_silu(values, gain_row):
    widened = values.astype(jnp.float32)
    mean_square = lax.optimization_barrier(jnp.mean(widened * widened, axis=-1, keepdims=True))
    return jax.nn.silu(widened * lax.rsqrt(mean_square + epsilon) * gain_row).astype(jnp.bfloat16)

def reference(latents, conv_weight, gain, bias):
    blocks, frames, height, columns, channels = latents.shape
    all_frames = blocks * frames
    current = latents.reshape(all_frames, height, columns, channels)
    for section_idx in range(conv_weight.shape[0]):
        activated = normed_silu(current, gain[section_idx])
        padded = jnp.pad(activated, ((2, 0), (1, 1), (1, 1), (0, 0)))
        total = jnp.zeros((all_frames * height * columns, channels), jnp.float32)
        for tap_t in range(3):
            for tap_r in range(3):
                for tap_c in range(3):
                    piece = padded[tap_t:tap_t + all_frames, tap_r:tap_r + height, tap_c:tap_c + columns]
                    total = total + jnp.dot(piece.reshape(-1, channels), conv_weight[section_idx, tap_t, tap_r, tap_c], preferred_element_type=jnp.float32)
        summed = current.astype(jnp.float32) + total.reshape(all_frames, height, columns, channels) + bias[section_idx]
        current = summed.astype(jnp.bfloat16)
    return current.reshape(latents.shape)
```

```python
import functools

import jax
import jax.numpy as jnp
from jax import lax
from jax.experimental import pallas as pl
from jax.experimental.pallas import tpu as pltpu
from jax.sharding import PartitionSpec as P

EPSILON = 1e-06
GROUP = 2


def kernel(
    sections, row_count, group,
    lat_ref, w_hbm, gain_ref, bias_ref, o_ref,
    weights, acts, incoming, outgoing, total,
    w_sem, lat_send, in_recv, out_send, halo_send, halo_recv, own_recv,
):
    frames, cols, ch = lat_ref.shape
    all_frames = sections * frames
    per_block = frames // group
    items = sections * per_block
    rows = group * cols
    section = lax.axis_index("section")
    row = lax.axis_index("rows")
    last = sections - 1

    place = (0, 2, 1)

    def weight_copy(i, j, k):
        return pltpu.make_async_copy(
            w_hbm.at[i, j, k],
            weights.at[i, pl.ds(place[j] * ch, ch), pl.ds(k * ch, ch)],
            w_sem.at[i, j, k],
        )

    for i in (2, 1, 0):
        for j in (1, 0, 2):
            for k in range(3):
                weight_copy(i, j, k).start()

    def weights_here(i):
        for j in (1, 0, 2):
            for k in range(3):
                weight_copy(i, j, k).wait()

    barrier = pltpu.get_barrier_semaphore()
    for peer in range(sections):
        @pl.when(section != peer)
        def _():
            pl.semaphore_signal(barrier, inc=1, device_id={"section": peer})

    @pl.when(row > 0)
    def _():
        pl.semaphore_signal(barrier, inc=1, device_id={"rows": row - 1})

    @pl.when(row < row_count - 1)
    def _():
        pl.semaphore_signal(barrier, inc=1, device_id={"rows": row + 1})

    acts[0:2] = jnp.zeros((2, cols, 3 * ch), jnp.bfloat16)

    @pl.when(row == 0)
    def _():
        acts[:, :, 0:ch] = jnp.zeros((all_frames + 2, cols, ch), jnp.bfloat16)

    @pl.when(row == row_count - 1)
    def _():
        acts[:, :, ch : 2 * ch] = jnp.zeros((all_frames + 2, cols, ch), jnp.bfloat16)

    @pl.when(section == 0)
    def _():
        incoming[0:frames] = lat_ref[...]

    greeted = (
        sections - 1 + jnp.where(row > 0, 1, 0) + jnp.where(row < row_count - 1, 1, 0)
    )
    pl.semaphore_wait(barrier, greeted)

    def lat_copy(part):
        return pltpu.make_async_remote_copy(
            lat_ref.at[pl.ds(part * group, group)],
            incoming.at[pl.ds(section * frames + part * group, group)],
            lat_send.at[part],
            in_recv.at[section * per_block + part],
            device_id={"section": 0},
        )

    @pl.when(section > 0)
    def _():
        for part in range(per_block):
            lat_copy(part).start()

    def pass_copy(item):
        t0 = item * group
        return pltpu.make_async_remote_copy(
            outgoing.at[pl.ds(t0, group)],
            incoming.at[pl.ds(t0, group)],
            out_send.at[item],
            in_recv.at[item],
            device_id={"section": lax.rem(section + 1, sections)},
        )

    def home_copy(item):
        t0 = item * group
        part = lax.rem(item, per_block)
        return pltpu.make_async_remote_copy(
            outgoing.at[pl.ds(t0, group)],
            o_ref.at[pl.ds(part * group, group)],
            out_send.at[item],
            own_recv.at[part],
            device_id={"section": item // per_block},
        )

    def halo_copy(item, side):
        t0 = item * group
        lane = ch if side == 0 else 0
        target = row - 1 if side == 0 else row + 1
        return pltpu.make_async_remote_copy(
            acts.at[pl.ds(t0 + 2, group), :, pl.ds(2 * ch, ch)],
            acts.at[pl.ds(t0 + 2, group), :, pl.ds(lane, ch)],
            halo_send.at[item, side],
            halo_recv.at[item, side],
            device_id={"rows": target},
        )

    def taps(index, count, i, low, high):
        lhs = acts[pl.ds(index, count), :, low:high].reshape(count * cols, high - low)
        return jnp.dot(lhs, weights[i, low:high, :], preferred_element_type=jnp.float32)

    def current_taps(t0, low, high):
        for i in (2, 1, 0):
            h = min(2 - i, group)
            if h < group:
                total[h * cols :, :] += taps(t0 + i + h, group - h, i, low, high)

    gain_row = gain_ref[...]
    bias_row = bias_ref[...]
    col_id = lax.rem(lax.broadcasted_iota(jnp.int32, (rows, ch), 0), cols)

    def step(item, carry):
        t0 = item * group

        @pl.when(item == 0)
        def _():
            total[...] = jnp.zeros((rows, 3 * ch), jnp.float32)

        @pl.when(item > 0)
        def _():
            h = min(2, group)
            total[0 : h * cols, :] = taps(t0, h, 0, 0, 3 * ch)
            if h < group:
                total[h * cols :, :] = jnp.zeros((rows - h * cols, 3 * ch), jnp.float32)
            total[0:cols, :] += taps(t0 + 1, 1, 1, 0, 3 * ch)

        @pl.when((section > 0) | (item >= per_block))
        def _():
            pass_copy(item).wait_recv()

        x = incoming[pl.ds(t0, group)].reshape(rows, ch).astype(jnp.float32)
        mean_square = jnp.mean(x * x, axis=-1, keepdims=True)
        v = x * lax.rsqrt(mean_square + EPSILON) * gain_row
        act = (v * jax.nn.sigmoid(v)).astype(jnp.bfloat16)
        acts[pl.ds(t0 + 2, group), :, 2 * ch : 3 * ch] = act.reshape(group, cols, ch)

        @pl.when(row > 0)
        def _():
            halo_copy(item, 0).start()

        @pl.when(row < row_count - 1)
        def _():
            halo_copy(item, 1).start()

        @pl.when(item == 0)
        def _():
            weights_here(2)
            weights_here(1)

        current_taps(t0, 2 * ch, 3 * ch)

        @pl.when(row < row_count - 1)
        def _():
            halo_copy(item, 0).wait_recv()

        @pl.when(row > 0)
        def _():
            halo_copy(item, 1).wait_recv()

        current_taps(t0, 0, 2 * ch)

        left = pltpu.roll(total[:, 0:ch], 1, 0)
        left = jnp.where(col_id == 0, 0.0, left)
        right = pltpu.roll(total[:, 2 * ch : 3 * ch], rows - 1, 0)
        right = jnp.where(col_id == cols - 1, 0.0, right)
        y = x + (left + total[:, ch : 2 * ch] + right) + bias_row
        y = y.astype(jnp.bfloat16).reshape(group, cols, ch)

        home = (section == last) & (item >= last * per_block)

        @pl.when(home)
        def _():
            o_ref[pl.ds(t0 - last * frames, group)] = y

        @pl.when(jnp.logical_not(home))
        def _():
            outgoing[pl.ds(t0, group)] = y

        @pl.when(section < last)
        def _():
            pass_copy(item).start()

        @pl.when((section == last) & (item < last * per_block))
        def _():
            home_copy(item).start()

        @pl.when(item == 0)
        def _():
            weights_here(0)

        return carry

    lax.fori_loop(0, items, step, 0)

    @pl.when(section > 0)
    def _():
        for part in range(per_block):
            lat_copy(part).wait_send()

    def finish(item, carry):
        @pl.when(row > 0)
        def _():
            halo_copy(item, 0).wait_send()

        @pl.when(row < row_count - 1)
        def _():
            halo_copy(item, 1).wait_send()

        @pl.when((section < last) | (item < last * per_block))
        def _():
            pass_copy(item).wait_send()

        return carry

    lax.fori_loop(0, items, finish, 0)

    @pl.when(section < last)
    def _():
        for part in range(per_block):
            home_copy(part).wait_recv()


def solution(mesh):
    sections = mesh.shape["section"]
    row_count = mesh.shape["rows"]

    def body(latents, conv_weight, gain, bias):
        _, frames, _, cols, ch = latents.shape
        group = GROUP
        all_frames = sections * frames
        per_block = frames // group
        items = sections * per_block
        rows = group * cols
        dma = pltpu.SemaphoreType.DMA
        vmem = pl.BlockSpec(memory_space=pltpu.VMEM)
        out = pl.pallas_call(
            functools.partial(kernel, sections, row_count, group),
            out_shape=jax.ShapeDtypeStruct((frames, cols, ch), jnp.bfloat16),
            in_specs=[vmem, pl.BlockSpec(memory_space=pl.ANY), vmem, vmem],
            out_specs=vmem,
            scratch_shapes=[
                pltpu.VMEM((3, 3 * ch, 3 * ch), jnp.bfloat16),
                pltpu.VMEM((all_frames + 2, cols, 3 * ch), jnp.bfloat16),
                pltpu.VMEM((all_frames, cols, ch), jnp.bfloat16),
                pltpu.VMEM((all_frames, cols, ch), jnp.bfloat16),
                pltpu.VMEM((rows, 3 * ch), jnp.float32),
                dma((3, 3, 3)),
                dma((per_block,)),
                dma((items,)),
                dma((items,)),
                dma((items, 2)),
                dma((items, 2)),
                dma((per_block,)),
            ],
            compiler_params=pltpu.CompilerParams(
                collective_id=0, has_side_effects=True, vmem_limit_bytes=48 * 2**20
            ),
            cost_estimate=pl.CostEstimate(
                flops=2 * all_frames * cols * 27 * ch * ch,
                bytes_accessed=27 * ch * ch * 2,
                transcendentals=all_frames * cols * ch,
            ),
        )(latents.reshape(frames, cols, ch), conv_weight[0], gain, bias)
        return out.reshape(latents.shape)

    in_specs = (
        P("section", None, "rows", None, None),
        P("section", None, None, None, None, None),
        P("section", None),
        P("section", None),
    )
    out_specs = P("section", None, "rows", None, None)
    return jax.shard_map(body, mesh=mesh, in_specs=in_specs, out_specs=out_specs, check_vma=False)
```

```python
import functools

import jax
import jax.numpy as jnp
from jax import lax
from jax.experimental import pallas as pl
from jax.experimental.pallas import tpu as pltpu
from jax.sharding import PartitionSpec as P

EPSILON = 1e-06
GROUP = 2


def kernel(
    sections, row_count, group,
    lat_ref, w_hbm, gain_hbm, bias_hbm, o_ref,
    weights, acts, incoming, outgoing, total, gain_ref, bias_ref,
    w_sem, small_sem, lat_send, in_recv, out_send, halo_send, halo_recv, own_recv,
):
    frames, cols, ch = lat_ref.shape
    all_frames = sections * frames
    per_block = frames // group
    items = sections * per_block
    rows = group * cols
    section = lax.axis_index("section")
    row = lax.axis_index("rows")
    last = sections - 1

    place = {
        (1, 0): 0, (1, 2): 1, (2, 0): 2, (2, 2): 3,
        (1, 1): 4, (2, 1): 5,
        (0, 0): 6, (0, 2): 7, (0, 1): 8,
    }
    own_taps = ((1, 1), (2, 1))
    halo_taps = ((1, 0), (1, 2), (2, 0), (2, 2))
    old_taps = ((0, 0), (0, 2), (0, 1))

    def weight_copy(i, j, k):
        return pltpu.make_async_copy(
            w_hbm.at[i, j, k],
            weights.at[pl.ds(place[i, j] * ch, ch), pl.ds(k * ch, ch)],
            w_sem.at[i, j, k],
        )

    def weights_here(taps):
        for i, j in taps:
            for k in range(3):
                weight_copy(i, j, k).wait()

    gain_copy = pltpu.make_async_copy(gain_hbm, gain_ref, small_sem.at[0])
    bias_copy = pltpu.make_async_copy(bias_hbm, bias_ref, small_sem.at[1])
    first_copy = pltpu.make_async_copy(
        lat_ref, incoming.at[pl.ds(0, frames)], small_sem.at[2]
    )

    @pl.when(section == 0)
    def _():
        first_copy.start()

    gain_copy.start()
    bias_copy.start()
    for i, j in own_taps + halo_taps + old_taps:
        for k in range(3):
            weight_copy(i, j, k).start()

    barrier = pltpu.get_barrier_semaphore()
    for peer in range(sections):
        @pl.when(section != peer)
        def _():
            pl.semaphore_signal(barrier, inc=1, device_id={"section": peer})

    @pl.when(row > 0)
    def _():
        pl.semaphore_signal(barrier, inc=1, device_id={"rows": row - 1})

    @pl.when(row < row_count - 1)
    def _():
        pl.semaphore_signal(barrier, inc=1, device_id={"rows": row + 1})

    acts[0:2] = jnp.zeros((2, cols, 3 * ch), jnp.bfloat16)

    @pl.when(row == 0)
    def _():
        acts[:, :, 0:ch] = jnp.zeros((all_frames + 2, cols, ch), jnp.bfloat16)

    @pl.when(row == row_count - 1)
    def _():
        acts[:, :, ch : 2 * ch] = jnp.zeros((all_frames + 2, cols, ch), jnp.bfloat16)

    greeted = (
        sections - 1 + jnp.where(row > 0, 1, 0) + jnp.where(row < row_count - 1, 1, 0)
    )
    pl.semaphore_wait(barrier, greeted)

    def lat_copy(part):
        return pltpu.make_async_remote_copy(
            lat_ref.at[pl.ds(part * group, group)],
            incoming.at[pl.ds(section * frames + part * group, group)],
            lat_send.at[part],
            in_recv.at[section * per_block + part],
            device_id={"section": 0},
        )

    @pl.when(section > 0)
    def _():
        for part in range(per_block):
            lat_copy(part).start()

    def pass_copy(item):
        t0 = item * group
        return pltpu.make_async_remote_copy(
            outgoing.at[pl.ds(t0, group)],
            incoming.at[pl.ds(t0, group)],
            out_send.at[item],
            in_recv.at[item],
            device_id={"section": lax.rem(section + 1, sections)},
        )

    def home_copy(item):
        t0 = item * group
        part = lax.rem(item, per_block)
        return pltpu.make_async_remote_copy(
            outgoing.at[pl.ds(t0, group)],
            o_ref.at[pl.ds(part * group, group)],
            out_send.at[item],
            own_recv.at[part],
            device_id={"section": item // per_block},
        )

    def halo_copy(item, side):
        t0 = item * group
        lane = ch if side == 0 else 0
        target = row - 1 if side == 0 else row + 1
        return pltpu.make_async_remote_copy(
            acts.at[pl.ds(t0 + 2, group), :, pl.ds(2 * ch, ch)],
            acts.at[pl.ds(t0 + 2, group), :, pl.ds(lane, ch)],
            halo_send.at[item, side],
            halo_recv.at[item, side],
            device_id={"rows": target},
        )

    def product(starts, low, high, top):
        parts = [
            acts[pl.ds(start, group), :, low:high].reshape(rows, high - low)
            for start in starts
        ]
        lhs = jnp.concatenate(parts, axis=-1)
        rhs = weights[top * ch : top * ch + lhs.shape[1], :]
        return jnp.dot(lhs, rhs, preferred_element_type=jnp.float32)

    gain_copy.wait()
    bias_copy.wait()
    gain_row = gain_ref[...]
    bias_row = bias_ref[...]

    @pl.when(section == 0)
    def _():
        first_copy.wait()

    col_id = lax.rem(lax.broadcasted_iota(jnp.int32, (rows, ch), 0), cols)

    def step(item, carry):
        t0 = item * group

        @pl.when(item > 0)
        def _():
            total[...] = product((t0,), 0, 3 * ch, 6)

        @pl.when((section > 0) | (item >= per_block))
        def _():
            pass_copy(item).wait_recv()

        x = incoming[pl.ds(t0, group)].reshape(rows, ch).astype(jnp.float32)
        mean_square = jnp.mean(x * x, axis=-1, keepdims=True)
        v = x * lax.rsqrt(mean_square + EPSILON) * gain_row
        act = (v * jax.nn.sigmoid(v)).astype(jnp.bfloat16)
        acts[pl.ds(t0 + 2, group), :, 2 * ch : 3 * ch] = act.reshape(group, cols, ch)

        @pl.when(row > 0)
        def _():
            halo_copy(item, 0).start()

        @pl.when(row < row_count - 1)
        def _():
            halo_copy(item, 1).start()

        @pl.when(item == 0)
        def _():
            weights_here(own_taps)

        own = product((t0 + 1, t0 + 2), 2 * ch, 3 * ch, 4)

        @pl.when(item == 0)
        def _():
            total[...] = own
            weights_here(halo_taps)

        @pl.when(item > 0)
        def _():
            total[...] += own

        @pl.when(row < row_count - 1)
        def _():
            halo_copy(item, 0).wait_recv()

        @pl.when(row > 0)
        def _():
            halo_copy(item, 1).wait_recv()

        summed = total[...] + product((t0 + 1, t0 + 2), 0, 2 * ch, 0)
        left = pltpu.roll(summed[:, 0:ch], 1, 0)
        left = jnp.where(col_id == 0, 0.0, left)
        right = pltpu.roll(summed[:, 2 * ch : 3 * ch], rows - 1, 0)
        right = jnp.where(col_id == cols - 1, 0.0, right)
        y = x + (left + summed[:, ch : 2 * ch] + right) + bias_row
        y = y.astype(jnp.bfloat16).reshape(group, cols, ch)

        home = (section == last) & (item >= last * per_block)

        @pl.when(home)
        def _():
            o_ref[pl.ds(t0 - last * frames, group)] = y

        @pl.when(jnp.logical_not(home))
        def _():
            outgoing[pl.ds(t0, group)] = y

        @pl.when(section < last)
        def _():
            pass_copy(item).start()

        @pl.when((section == last) & (item < last * per_block))
        def _():
            home_copy(item).start()

        @pl.when(item == 0)
        def _():
            weights_here(old_taps)

        return carry

    lax.fori_loop(0, items, step, 0)

    @pl.when(section > 0)
    def _():
        for part in range(per_block):
            lat_copy(part).wait_send()

    def finish(item, carry):
        @pl.when(row > 0)
        def _():
            halo_copy(item, 0).wait_send()

        @pl.when(row < row_count - 1)
        def _():
            halo_copy(item, 1).wait_send()

        @pl.when((section < last) | (item < last * per_block))
        def _():
            pass_copy(item).wait_send()

        return carry

    lax.fori_loop(0, items, finish, 0)

    @pl.when(section < last)
    def _():
        for part in range(per_block):
            home_copy(part).wait_recv()


def solution(mesh):
    sections = mesh.shape["section"]
    row_count = mesh.shape["rows"]

    def body(latents, conv_weight, gain, bias):
        _, frames, _, cols, ch = latents.shape
        group = GROUP
        all_frames = sections * frames
        per_block = frames // group
        items = sections * per_block
        rows = group * cols
        dma = pltpu.SemaphoreType.DMA
        vmem = pl.BlockSpec(memory_space=pltpu.VMEM)
        out = pl.pallas_call(
            functools.partial(kernel, sections, row_count, group),
            out_shape=jax.ShapeDtypeStruct((frames, cols, ch), jnp.bfloat16),
            in_specs=[pl.BlockSpec(memory_space=pl.ANY)] * 4,
            out_specs=vmem,
            scratch_shapes=[
                pltpu.VMEM((9 * ch, 3 * ch), jnp.bfloat16),
                pltpu.VMEM((all_frames + 2, cols, 3 * ch), jnp.bfloat16),
                pltpu.VMEM((all_frames, cols, ch), jnp.bfloat16),
                pltpu.VMEM((all_frames, cols, ch), jnp.bfloat16),
                pltpu.VMEM((rows, 3 * ch), jnp.float32),
                pltpu.VMEM((1, ch), jnp.float32),
                pltpu.VMEM((1, ch), jnp.float32),
                dma((3, 3, 3)),
                dma((3,)),
                dma((per_block,)),
                dma((items,)),
                dma((items,)),
                dma((items, 2)),
                dma((items, 2)),
                dma((per_block,)),
            ],
            compiler_params=pltpu.CompilerParams(
                collective_id=0, has_side_effects=True, vmem_limit_bytes=60 * 2**20
            ),
            cost_estimate=pl.CostEstimate(
                flops=2 * all_frames * cols * 27 * ch * ch,
                bytes_accessed=27 * ch * ch * 2,
                transcendentals=all_frames * cols * ch,
            ),
        )(latents.reshape(frames, cols, ch), conv_weight[0], gain, bias)
        return out.reshape(latents.shape)

    in_specs = (
        P("section", None, "rows", None, None),
        P("section", None, None, None, None, None),
        P("section", None),
        P("section", None),
    )
    out_specs = P("section", None, "rows", None, None)
    return jax.shard_map(body, mesh=mesh, in_specs=in_specs, out_specs=out_specs, check_vma=False)
```

```python
import functools

import jax
import jax.numpy as jnp
from jax import lax
from jax.experimental import pallas as pl
from jax.experimental.pallas import tpu as pltpu
from jax.sharding import PartitionSpec as P

EPSILON = 1e-06
GROUP = 1


def kernel(
    sections, row_count, group,
    lat_ref, w_hbm, gain_hbm, bias_hbm, o_ref,
    weights, acts, incoming, outgoing, total, gain_ref, bias_ref,
    w_sem, small_sem, lat_send, in_recv, out_send, halo_send, halo_recv, own_recv,
):
    frames, cols, ch = lat_ref.shape
    all_frames = sections * frames
    per_block = frames // group
    items = sections * per_block
    rows = group * cols
    section = lax.axis_index("section")
    row = lax.axis_index("rows")
    last = sections - 1

    own_taps = ((2, 1),)
    halo_taps = ((2, 0), (2, 2))
    old_taps = ((0, 0), (0, 2), (0, 1), (1, 0), (1, 2), (1, 1))
    place = {tap: at for at, tap in enumerate(own_taps + halo_taps + old_taps)}

    def weight_copy(i, j, k):
        return pltpu.make_async_copy(
            w_hbm.at[i, j, k],
            weights.at[pl.ds(place[i, j] * ch, ch), pl.ds(k * ch, ch)],
            w_sem.at[i, j, k],
        )

    def weights_here(taps):
        for i, j in taps:
            for k in range(3):
                weight_copy(i, j, k).wait()

    gain_copy = pltpu.make_async_copy(gain_hbm, gain_ref, small_sem.at[0])
    bias_copy = pltpu.make_async_copy(bias_hbm, bias_ref, small_sem.at[1])
    first_copy = pltpu.make_async_copy(
        lat_ref, incoming.at[pl.ds(0, frames)], small_sem.at[2]
    )

    @pl.when(section == 0)
    def _():
        first_copy.start()

    gain_copy.start()
    bias_copy.start()
    for i, j in own_taps + halo_taps + old_taps:
        for k in range(3):
            weight_copy(i, j, k).start()

    barrier = pltpu.get_barrier_semaphore()
    for peer in range(sections):
        @pl.when(section != peer)
        def _():
            pl.semaphore_signal(barrier, inc=1, device_id={"section": peer})

    @pl.when(row > 0)
    def _():
        pl.semaphore_signal(barrier, inc=1, device_id={"rows": row - 1})

    @pl.when(row < row_count - 1)
    def _():
        pl.semaphore_signal(barrier, inc=1, device_id={"rows": row + 1})

    acts[0:2] = jnp.zeros((2, cols, 3 * ch), jnp.bfloat16)

    @pl.when(row == 0)
    def _():
        acts[:, :, 0:ch] = jnp.zeros((all_frames + 2, cols, ch), jnp.bfloat16)

    @pl.when(row == row_count - 1)
    def _():
        acts[:, :, ch : 2 * ch] = jnp.zeros((all_frames + 2, cols, ch), jnp.bfloat16)

    greeted = (
        sections - 1 + jnp.where(row > 0, 1, 0) + jnp.where(row < row_count - 1, 1, 0)
    )
    pl.semaphore_wait(barrier, greeted)

    def lat_copy(part):
        return pltpu.make_async_remote_copy(
            lat_ref.at[pl.ds(part * group, group)],
            incoming.at[pl.ds(section * frames + part * group, group)],
            lat_send.at[part],
            in_recv.at[section * per_block + part],
            device_id={"section": 0},
        )

    @pl.when(section > 0)
    def _():
        for part in range(per_block):
            lat_copy(part).start()

    def pass_copy(item):
        t0 = item * group
        return pltpu.make_async_remote_copy(
            outgoing.at[pl.ds(t0, group)],
            incoming.at[pl.ds(t0, group)],
            out_send.at[item],
            in_recv.at[item],
            device_id={"section": lax.rem(section + 1, sections)},
        )

    def home_copy(item):
        t0 = item * group
        part = lax.rem(item, per_block)
        return pltpu.make_async_remote_copy(
            outgoing.at[pl.ds(t0, group)],
            o_ref.at[pl.ds(part * group, group)],
            out_send.at[item],
            own_recv.at[part],
            device_id={"section": item // per_block},
        )

    def halo_copy(item, side):
        t0 = item * group
        lane = ch if side == 0 else 0
        target = row - 1 if side == 0 else row + 1
        return pltpu.make_async_remote_copy(
            acts.at[pl.ds(t0 + 2, group), :, pl.ds(2 * ch, ch)],
            acts.at[pl.ds(t0 + 2, group), :, pl.ds(lane, ch)],
            halo_send.at[item, side],
            halo_recv.at[item, side],
            device_id={"rows": target},
        )

    def product(starts, low, high, top):
        parts = [
            acts[pl.ds(start, group), :, low:high].reshape(rows, high - low)
            for start in starts
        ]
        lhs = jnp.concatenate(parts, axis=-1)
        rhs = weights[top * ch : top * ch + lhs.shape[1], :]
        return jnp.dot(lhs, rhs, preferred_element_type=jnp.float32)

    gain_copy.wait()
    bias_copy.wait()
    gain_row = gain_ref[...]
    bias_row = bias_ref[...]

    @pl.when(section == 0)
    def _():
        first_copy.wait()

    col_id = lax.rem(lax.broadcasted_iota(jnp.int32, (rows, ch), 0), cols)

    def step(item, carry):
        t0 = item * group

        @pl.when((section > 0) | (item >= per_block))
        def _():
            pass_copy(item).wait_recv()

        x = incoming[pl.ds(t0, group)].reshape(rows, ch).astype(jnp.float32)
        mean_square = jnp.mean(x * x, axis=-1, keepdims=True)
        v = x * lax.rsqrt(mean_square + EPSILON) * gain_row
        act = (v * jax.nn.sigmoid(v)).astype(jnp.bfloat16)
        acts[pl.ds(t0 + 2, group), :, 2 * ch : 3 * ch] = act.reshape(group, cols, ch)

        @pl.when(row > 0)
        def _():
            halo_copy(item, 0).start()

        @pl.when(row < row_count - 1)
        def _():
            halo_copy(item, 1).start()

        @pl.when(item == 0)
        def _():
            weights_here(own_taps)

        total[...] = product((t0 + 2,), 2 * ch, 3 * ch, 0)

        @pl.when(item == 0)
        def _():
            weights_here(halo_taps)

        @pl.when(item > 0)
        def _():
            total[...] += product((t0, t0 + 1), 0, 3 * ch, 3)

        @pl.when(row < row_count - 1)
        def _():
            halo_copy(item, 0).wait_recv()

        @pl.when(row > 0)
        def _():
            halo_copy(item, 1).wait_recv()

        summed = total[...] + product((t0 + 2,), 0, 2 * ch, 1)
        left = pltpu.roll(summed[:, 0:ch], 1, 0)
        left = jnp.where(col_id == 0, 0.0, left)
        right = pltpu.roll(summed[:, 2 * ch : 3 * ch], rows - 1, 0)
        right = jnp.where(col_id == cols - 1, 0.0, right)
        y = x + (left + summed[:, ch : 2 * ch] + right) + bias_row
        y = y.astype(jnp.bfloat16).reshape(group, cols, ch)

        home = (section == last) & (item >= last * per_block)

        @pl.when(home)
        def _():
            o_ref[pl.ds(t0 - last * frames, group)] = y

        @pl.when(jnp.logical_not(home))
        def _():
            outgoing[pl.ds(t0, group)] = y

        @pl.when(section < last)
        def _():
            pass_copy(item).start()

        @pl.when((section == last) & (item < last * per_block))
        def _():
            home_copy(item).start()

        @pl.when(item == 0)
        def _():
            weights_here(old_taps)

        return carry

    lax.fori_loop(0, items, step, 0)

    @pl.when(section > 0)
    def _():
        for part in range(per_block):
            lat_copy(part).wait_send()

    def finish(item, carry):
        @pl.when(row > 0)
        def _():
            halo_copy(item, 0).wait_send()

        @pl.when(row < row_count - 1)
        def _():
            halo_copy(item, 1).wait_send()

        @pl.when((section < last) | (item < last * per_block))
        def _():
            pass_copy(item).wait_send()

        return carry

    lax.fori_loop(0, items, finish, 0)

    @pl.when(section < last)
    def _():
        for part in range(per_block):
            home_copy(part).wait_recv()


def solution(mesh):
    sections = mesh.shape["section"]
    row_count = mesh.shape["rows"]

    def body(latents, conv_weight, gain, bias):
        _, frames, _, cols, ch = latents.shape
        group = GROUP
        all_frames = sections * frames
        per_block = frames // group
        items = sections * per_block
        rows = group * cols
        dma = pltpu.SemaphoreType.DMA
        vmem = pl.BlockSpec(memory_space=pltpu.VMEM)
        out = pl.pallas_call(
            functools.partial(kernel, sections, row_count, group),
            out_shape=jax.ShapeDtypeStruct((frames, cols, ch), jnp.bfloat16),
            in_specs=[pl.BlockSpec(memory_space=pltpu.HBM)] * 4,
            out_specs=vmem,
            scratch_shapes=[
                pltpu.VMEM((9 * ch, 3 * ch), jnp.bfloat16),
                pltpu.VMEM((all_frames + 2, cols, 3 * ch), jnp.bfloat16),
                pltpu.VMEM((all_frames, cols, ch), jnp.bfloat16),
                pltpu.VMEM((all_frames, cols, ch), jnp.bfloat16),
                pltpu.VMEM((rows, 3 * ch), jnp.float32),
                pltpu.VMEM((1, ch), jnp.float32),
                pltpu.VMEM((1, ch), jnp.float32),
                dma((3, 3, 3)),
                dma((3,)),
                dma((per_block,)),
                dma((items,)),
                dma((items,)),
                dma((items, 2)),
                dma((items, 2)),
                dma((per_block,)),
            ],
            compiler_params=pltpu.CompilerParams(
                collective_id=0, has_side_effects=True, vmem_limit_bytes=58 * 2**20
            ),
            cost_estimate=pl.CostEstimate(
                flops=2 * all_frames * cols * 27 * ch * ch,
                bytes_accessed=27 * ch * ch * 2,
                transcendentals=all_frames * cols * ch,
            ),
        )(latents.reshape(frames, cols, ch), conv_weight[0], gain, bias)
        return out.reshape(latents.shape)

    in_specs = (
        P("section", None, "rows", None, None),
        P("section", None, None, None, None, None),
        P("section", None),
        P("section", None),
    )
    out_specs = P("section", None, "rows", None, None)
    return jax.shard_map(body, mesh=mesh, in_specs=in_specs, out_specs=out_specs, check_vma=False)
```

```python
import functools
import math

import jax
import jax.numpy as jnp
from jax import lax
from jax.experimental import pallas as pl
from jax.experimental.pallas import tpu as pltpu
from jax.sharding import PartitionSpec as P

EPSILON = 1e-06
GROUP = 2


def kernel(
    sections, row_count, side, group,
    lat_ref, w_hbm, gain_hbm, bias_hbm, o_ref,
    weights, acts, incoming, outgoing, total, gain_ref, bias_ref,
    w_sem, small_sem, lat_send, in_recv, out_send, halo_send, halo_recv, own_recv,
):
    frames, cols, ch = lat_ref.shape
    all_frames = sections * frames
    per_block = frames // group
    items = sections * per_block
    rows = group * cols
    section = lax.axis_index("section")
    place_at = lax.axis_index("rows")
    last = sections - 1

    def dealt(index):
        chip = index // 2
        line = chip // side
        along = chip % side
        turned = along + (line % 2) * (side - 1 - 2 * along)
        return (line * side + turned) * 2 + index % 2

    row = dealt(place_at)
    stays = row == place_at

    barrier = pltpu.get_barrier_semaphore()
    for peer in range(sections):
        @pl.when(section != peer)
        def _():
            pl.semaphore_signal(barrier, inc=1, device_id={"section": peer})

        @pl.when(jnp.logical_not(stays))
        def _():
            pl.semaphore_signal(
                barrier, inc=1, device_id={"section": peer, "rows": row}
            )

    @pl.when(row > 0)
    def _():
        pl.semaphore_signal(barrier, inc=1, device_id={"rows": dealt(row - 1)})

    @pl.when(row < row_count - 1)
    def _():
        pl.semaphore_signal(barrier, inc=1, device_id={"rows": dealt(row + 1)})

    place = {
        (1, 0): 0, (1, 2): 1, (2, 0): 2, (2, 2): 3,
        (1, 1): 4, (2, 1): 5,
        (0, 0): 6, (0, 2): 7, (0, 1): 8,
    }
    own_taps = ((1, 1), (2, 1))
    halo_taps = ((1, 0), (1, 2), (2, 0), (2, 2))
    old_taps = ((0, 0), (0, 2), (0, 1))

    def weight_copy(i, j, k):
        return pltpu.make_async_copy(
            w_hbm.at[i, j, k],
            weights.at[pl.ds(place[i, j] * ch, ch), pl.ds(k * ch, ch)],
            w_sem.at[i, j, k],
        )

    def weights_here(taps):
        for i, j in taps:
            for k in range(3):
                weight_copy(i, j, k).wait()

    gain_copy = pltpu.make_async_copy(gain_hbm, gain_ref, small_sem.at[0])
    bias_copy = pltpu.make_async_copy(bias_hbm, bias_ref, small_sem.at[1])
    first_copy = pltpu.make_async_copy(
        lat_ref, incoming.at[pl.ds(0, frames)], small_sem.at[2]
    )

    @pl.when((section == 0) & stays)
    def _():
        first_copy.start()

    gain_copy.start()
    bias_copy.start()
    for i, j in own_taps + halo_taps:
        for k in range(3):
            weight_copy(i, j, k).start()

    acts[0:2] = jnp.zeros((2, cols, 3 * ch), jnp.bfloat16)

    @pl.when(row == 0)
    def _():
        acts[:, :, 0:ch] = jnp.zeros((all_frames + 2, cols, ch), jnp.bfloat16)

    @pl.when(row == row_count - 1)
    def _():
        acts[:, :, ch : 2 * ch] = jnp.zeros((all_frames + 2, cols, ch), jnp.bfloat16)

    greeted = (
        sections - 1
        + jnp.where(stays, 0, sections)
        + jnp.where(row > 0, 1, 0)
        + jnp.where(row < row_count - 1, 1, 0)
    )
    pl.semaphore_wait(barrier, greeted)

    def lat_copy(part):
        return pltpu.make_async_remote_copy(
            lat_ref.at[pl.ds(part * group, group)],
            incoming.at[pl.ds(section * frames + part * group, group)],
            lat_send.at[part],
            in_recv.at[section * per_block + part],
            device_id={"section": 0, "rows": row},
        )

    sends_in = (section > 0) | jnp.logical_not(stays)

    @pl.when(sends_in)
    def _():
        for part in range(per_block):
            lat_copy(part).start()

    def pass_copy(item):
        t0 = item * group
        return pltpu.make_async_remote_copy(
            outgoing.at[pl.ds(t0, group)],
            incoming.at[pl.ds(t0, group)],
            out_send.at[item],
            in_recv.at[item],
            device_id={"section": lax.rem(section + 1, sections)},
        )

    def home_copy(item):
        t0 = item * group
        part = lax.rem(item, per_block)
        return pltpu.make_async_remote_copy(
            outgoing.at[pl.ds(t0, group)],
            o_ref.at[pl.ds(part * group, group)],
            out_send.at[item],
            own_recv.at[part],
            device_id={"section": item // per_block, "rows": row},
        )

    def halo_copy(item, way):
        t0 = item * group
        lane = ch if way == 0 else 0
        target = dealt(row - 1 if way == 0 else row + 1)
        return pltpu.make_async_remote_copy(
            acts.at[pl.ds(t0 + 2, group), :, pl.ds(2 * ch, ch)],
            acts.at[pl.ds(t0 + 2, group), :, pl.ds(lane, ch)],
            halo_send.at[item, way],
            halo_recv.at[item, way],
            device_id={"rows": target},
        )

    def product(starts, low, high, top):
        parts = [
            acts[pl.ds(start, group), :, low:high].reshape(rows, high - low)
            for start in starts
        ]
        lhs = jnp.concatenate(parts, axis=-1)
        rhs = weights[top * ch : top * ch + lhs.shape[1], :]
        return jnp.dot(lhs, rhs, preferred_element_type=jnp.float32)

    gain_copy.wait()
    bias_copy.wait()
    gain_row = gain_ref[...]
    bias_row = bias_ref[...]

    @pl.when((section == 0) & stays)
    def _():
        first_copy.wait()

    col_id = lax.rem(lax.broadcasted_iota(jnp.int32, (rows, ch), 0), cols)

    def step(item, carry):
        t0 = item * group

        @pl.when(sends_in | (item >= per_block))
        def _():
            pass_copy(item).wait_recv()

        x = incoming[pl.ds(t0, group)].reshape(rows, ch).astype(jnp.float32)
        mean_square = jnp.mean(x * x, axis=-1, keepdims=True)
        v = x * lax.rsqrt(mean_square + EPSILON) * gain_row
        act = (v * jax.nn.sigmoid(v)).astype(jnp.bfloat16)
        acts[pl.ds(t0 + 2, group), :, 2 * ch : 3 * ch] = act.reshape(group, cols, ch)

        @pl.when(row > 0)
        def _():
            halo_copy(item, 0).start()

        @pl.when(row < row_count - 1)
        def _():
            halo_copy(item, 1).start()

        @pl.when(item == 0)
        def _():
            weights_here(own_taps)

        own = product((t0 + 1, t0 + 2), 2 * ch, 3 * ch, 4)

        @pl.when(item == 0)
        def _():
            total[...] = own
            weights_here(halo_taps)
            for i, j in old_taps:
                for k in range(3):
                    weight_copy(i, j, k).start()

        @pl.when(item > 0)
        def _():
            total[...] = own + product((t0,), 0, 3 * ch, 6)

        @pl.when(row < row_count - 1)
        def _():
            halo_copy(item, 0).wait_recv()

        @pl.when(row > 0)
        def _():
            halo_copy(item, 1).wait_recv()

        summed = total[...] + product((t0 + 1, t0 + 2), 0, 2 * ch, 0)
        left = pltpu.roll(summed[:, 0:ch], 1, 0)
        left = jnp.where(col_id == 0, 0.0, left)
        right = pltpu.roll(summed[:, 2 * ch : 3 * ch], rows - 1, 0)
        right = jnp.where(col_id == cols - 1, 0.0, right)
        y = x + (left + summed[:, ch : 2 * ch] + right) + bias_row
        y = y.astype(jnp.bfloat16).reshape(group, cols, ch)

        home = (section == last) & (item >= last * per_block) & stays

        @pl.when(home)
        def _():
            o_ref[pl.ds(t0 - last * frames, group)] = y

        @pl.when(jnp.logical_not(home))
        def _():
            outgoing[pl.ds(t0, group)] = y

        @pl.when(section < last)
        def _():
            pass_copy(item).start()

        @pl.when((section == last) & jnp.logical_not(home))
        def _():
            home_copy(item).start()

        @pl.when(item == 0)
        def _():
            weights_here(old_taps)

        return carry

    lax.fori_loop(0, items, step, 0)

    @pl.when(sends_in)
    def _():
        for part in range(per_block):
            lat_copy(part).wait_send()

    def finish(item, carry):
        @pl.when(row > 0)
        def _():
            halo_copy(item, 0).wait_send()

        @pl.when(row < row_count - 1)
        def _():
            halo_copy(item, 1).wait_send()

        @pl.when((section < last) | (item < last * per_block) | jnp.logical_not(stays))
        def _():
            pass_copy(item).wait_send()

        return carry

    lax.fori_loop(0, items, finish, 0)

    @pl.when((section < last) | jnp.logical_not(stays))
    def _():
        for part in range(per_block):
            home_copy(part).wait_recv()


def solution(mesh):
    sections = mesh.shape["section"]
    row_count = mesh.shape["rows"]
    side = math.isqrt(row_count // 2)
    if 2 * side * side != row_count:
        side = 1

    def body(latents, conv_weight, gain, bias):
        _, frames, _, cols, ch = latents.shape
        group = GROUP
        all_frames = sections * frames
        per_block = frames // group
        items = sections * per_block
        rows = group * cols
        dma = pltpu.SemaphoreType.DMA
        vmem = pl.BlockSpec(memory_space=pltpu.VMEM)
        out = pl.pallas_call(
            functools.partial(kernel, sections, row_count, side, group),
            out_shape=jax.ShapeDtypeStruct((frames, cols, ch), jnp.bfloat16),
            in_specs=[pl.BlockSpec(memory_space=pl.ANY)] * 4,
            out_specs=vmem,
            scratch_shapes=[
                pltpu.VMEM((9 * ch, 3 * ch), jnp.bfloat16),
                pltpu.VMEM((all_frames + 2, cols, 3 * ch), jnp.bfloat16),
                pltpu.VMEM((all_frames, cols, ch), jnp.bfloat16),
                pltpu.VMEM((all_frames, cols, ch), jnp.bfloat16),
                pltpu.VMEM((rows, 3 * ch), jnp.float32),
                pltpu.VMEM((1, ch), jnp.float32),
                pltpu.VMEM((1, ch), jnp.float32),
                dma((3, 3, 3)),
                dma((3,)),
                dma((per_block,)),
                dma((items,)),
                dma((items,)),
                dma((items, 2)),
                dma((items, 2)),
                dma((per_block,)),
            ],
            compiler_params=pltpu.CompilerParams(
                collective_id=0, has_side_effects=True, vmem_limit_bytes=60 * 2**20
            ),
            cost_estimate=pl.CostEstimate(
                flops=2 * all_frames * cols * 27 * ch * ch,
                bytes_accessed=27 * ch * ch * 2,
                transcendentals=all_frames * cols * ch,
            ),
        )(latents.reshape(frames, cols, ch), conv_weight[0], gain, bias)
        return out.reshape(latents.shape)

    in_specs = (
        P("section", None, "rows", None, None),
        P("section", None, None, None, None, None),
        P("section", None),
        P("section", None),
    )
    out_specs = P("section", None, "rows", None, None)
    return jax.shard_map(body, mesh=mesh, in_specs=in_specs, out_specs=out_specs, check_vma=False)
```

```python
import functools

import jax
import jax.numpy as jnp
from jax import lax
from jax.experimental import pallas as pl
from jax.experimental.pallas import tpu as pltpu
from jax.sharding import PartitionSpec as P

EPSILON = 1e-06
GROUP = 2


def kernel(
    sections, row_count, group,
    lat_ref, w_hbm, gain_hbm, bias_hbm, o_ref,
    weights, acts, incoming, outgoing, total, gain_ref, bias_ref,
    w_sem, small_sem, lat_send, in_recv, out_send, halo_send, halo_recv, own_recv,
):
    frames, cols, ch = lat_ref.shape
    all_frames = sections * frames
    per_block = frames // group
    items = sections * per_block
    rows = group * cols
    section = lax.axis_index("section")
    row = lax.axis_index("rows")
    last = sections - 1

    barrier = pltpu.get_barrier_semaphore()
    for peer in range(sections):
        @pl.when(section != peer)
        def _():
            pl.semaphore_signal(barrier, inc=1, device_id={"section": peer})

    @pl.when(row > 0)
    def _():
        pl.semaphore_signal(barrier, inc=1, device_id={"rows": row - 1})

    @pl.when(row < row_count - 1)
    def _():
        pl.semaphore_signal(barrier, inc=1, device_id={"rows": row + 1})

    place = {
        (1, 0): 0, (1, 2): 1, (2, 0): 2, (2, 2): 3,
        (1, 1): 4, (2, 1): 5,
        (0, 0): 6, (0, 2): 7, (0, 1): 8,
    }
    own_taps = ((1, 1), (2, 1))
    halo_taps = ((1, 0), (1, 2), (2, 0), (2, 2))
    old_taps = ((0, 0), (0, 2), (0, 1))

    def weight_copy(i, j, k):
        return pltpu.make_async_copy(
            w_hbm.at[i, j, k],
            weights.at[pl.ds(place[i, j] * ch, ch), pl.ds(k * ch, ch)],
            w_sem.at[i, j, k],
        )

    def weights_start(taps):
        for i, j in taps:
            for k in range(3):
                weight_copy(i, j, k).start(priority=1)

    def weights_here(taps):
        for i, j in taps:
            for k in range(3):
                weight_copy(i, j, k).wait()

    gain_copy = pltpu.make_async_copy(gain_hbm, gain_ref, small_sem.at[0])
    bias_copy = pltpu.make_async_copy(bias_hbm, bias_ref, small_sem.at[1])
    first_copy = pltpu.make_async_copy(
        lat_ref, incoming.at[pl.ds(0, frames)], small_sem.at[2]
    )

    @pl.when(section == 0)
    def _():
        first_copy.start()

    gain_copy.start()
    bias_copy.start()
    weights_start(own_taps)

    @pl.when(section > 0)
    def _():
        weights_start(halo_taps + old_taps)


    acts[0:2] = jnp.zeros((2, cols, 3 * ch), jnp.bfloat16)

    @pl.when(row == 0)
    def _():
        acts[:, :, 0:ch] = jnp.zeros((all_frames + 2, cols, ch), jnp.bfloat16)

    @pl.when(row == row_count - 1)
    def _():
        acts[:, :, ch : 2 * ch] = jnp.zeros((all_frames + 2, cols, ch), jnp.bfloat16)

    greeted = (
        sections - 1 + jnp.where(row > 0, 1, 0) + jnp.where(row < row_count - 1, 1, 0)
    )
    pl.semaphore_wait(barrier, greeted)

    def lat_copy(part):
        return pltpu.make_async_remote_copy(
            lat_ref.at[pl.ds(part * group, group)],
            incoming.at[pl.ds(section * frames + part * group, group)],
            lat_send.at[part],
            in_recv.at[section * per_block + part],
            device_id={"section": 0},
        )

    @pl.when(section > 0)
    def _():
        for part in range(per_block):
            lat_copy(part).start()

    def pass_copy(item):
        t0 = item * group
        return pltpu.make_async_remote_copy(
            outgoing.at[pl.ds(t0, group)],
            incoming.at[pl.ds(t0, group)],
            out_send.at[item],
            in_recv.at[item],
            device_id={"section": lax.rem(section + 1, sections)},
        )

    def home_copy(item):
        t0 = item * group
        part = lax.rem(item, per_block)
        return pltpu.make_async_remote_copy(
            outgoing.at[pl.ds(t0, group)],
            o_ref.at[pl.ds(part * group, group)],
            out_send.at[item],
            own_recv.at[part],
            device_id={"section": item // per_block},
        )

    def halo_copy(item, side):
        t0 = item * group
        lane = ch if side == 0 else 0
        target = row - 1 if side == 0 else row + 1
        return pltpu.make_async_remote_copy(
            acts.at[pl.ds(t0 + 2, group), :, pl.ds(2 * ch, ch)],
            acts.at[pl.ds(t0 + 2, group), :, pl.ds(lane, ch)],
            halo_send.at[item, side],
            halo_recv.at[item, side],
            device_id={"rows": target},
        )

    def product(starts, low, high, top):
        parts = [
            acts[pl.ds(start, group), :, low:high].reshape(rows, high - low)
            for start in starts
        ]
        lhs = jnp.concatenate(parts, axis=-1)
        rhs = weights[top * ch : top * ch + lhs.shape[1], :]
        return jnp.dot(lhs, rhs, preferred_element_type=jnp.float32)

    gain_copy.wait()
    bias_copy.wait()
    gain_row = gain_ref[...]
    bias_row = bias_ref[...]

    @pl.when(section == 0)
    def _():
        first_copy.wait()

    col_id = lax.rem(lax.broadcasted_iota(jnp.int32, (rows, ch), 0), cols)

    def step(item, carry):
        t0 = item * group

        @pl.when((section > 0) | (item >= per_block))
        def _():
            pass_copy(item).wait_recv()

        x = incoming[pl.ds(t0, group)].reshape(rows, ch).astype(jnp.float32)
        mean_square = jnp.mean(x * x, axis=-1, keepdims=True)
        v = x * lax.rsqrt(mean_square + EPSILON) * gain_row
        act = (v * jax.nn.sigmoid(v)).astype(jnp.bfloat16)
        acts[pl.ds(t0 + 2, group), :, 2 * ch : 3 * ch] = act.reshape(group, cols, ch)

        @pl.when(row > 0)
        def _():
            halo_copy(item, 0).start()

        @pl.when(row < row_count - 1)
        def _():
            halo_copy(item, 1).start()

        @pl.when((item == 0) & (section == 0))
        def _():
            weights_start(halo_taps)

        @pl.when(item == 0)
        def _():
            weights_here(own_taps)

        @pl.when(item == 1)
        def _():
            weights_here(old_taps)

        own = product((t0 + 1, t0 + 2), 2 * ch, 3 * ch, 4)

        @pl.when(item == 0)
        def _():
            total[...] = own
            weights_here(halo_taps)

        @pl.when(item > 0)
        def _():
            total[...] = own + product((t0,), 0, 3 * ch, 6)

        @pl.when(row < row_count - 1)
        def _():
            halo_copy(item, 0).wait_recv()

        @pl.when(row > 0)
        def _():
            halo_copy(item, 1).wait_recv()

        summed = total[...] + product((t0 + 1, t0 + 2), 0, 2 * ch, 0)
        left = pltpu.roll(summed[:, 0:ch], 1, 0)
        left = jnp.where(col_id == 0, 0.0, left)
        right = pltpu.roll(summed[:, 2 * ch : 3 * ch], rows - 1, 0)
        right = jnp.where(col_id == cols - 1, 0.0, right)
        y = x + (left + summed[:, ch : 2 * ch] + right) + bias_row
        y = y.astype(jnp.bfloat16).reshape(group, cols, ch)

        home = (section == last) & (item >= last * per_block)

        @pl.when(home)
        def _():
            o_ref[pl.ds(t0 - last * frames, group)] = y

        @pl.when(jnp.logical_not(home))
        def _():
            outgoing[pl.ds(t0, group)] = y

        @pl.when(section < last)
        def _():
            pass_copy(item).start()

        @pl.when((section == last) & (item < last * per_block))
        def _():
            home_copy(item).start()

        @pl.when((item == 0) & (section == 0))
        def _():
            weights_start(old_taps)

        return carry

    lax.fori_loop(0, items, step, 0)

    @pl.when(section > 0)
    def _():
        for part in range(per_block):
            lat_copy(part).wait_send()

    def finish(item, carry):
        @pl.when(row > 0)
        def _():
            halo_copy(item, 0).wait_send()

        @pl.when(row < row_count - 1)
        def _():
            halo_copy(item, 1).wait_send()

        @pl.when((section < last) | (item < last * per_block))
        def _():
            pass_copy(item).wait_send()

        return carry

    lax.fori_loop(0, items, finish, 0)

    @pl.when(section < last)
    def _():
        for part in range(per_block):
            home_copy(part).wait_recv()


def solution(mesh):
    sections = mesh.shape["section"]
    row_count = mesh.shape["rows"]

    def body(latents, conv_weight, gain, bias):
        _, frames, _, cols, ch = latents.shape
        group = GROUP
        all_frames = sections * frames
        per_block = frames // group
        items = sections * per_block
        rows = group * cols
        dma = pltpu.SemaphoreType.DMA
        vmem = pl.BlockSpec(memory_space=pltpu.VMEM)
        out = pl.pallas_call(
            functools.partial(kernel, sections, row_count, group),
            out_shape=jax.ShapeDtypeStruct((frames, cols, ch), jnp.bfloat16),
            in_specs=[pl.BlockSpec(memory_space=pl.ANY)] * 4,
            out_specs=vmem,
            scratch_shapes=[
                pltpu.VMEM((9 * ch, 3 * ch), jnp.bfloat16),
                pltpu.VMEM((all_frames + 2, cols, 3 * ch), jnp.bfloat16),
                pltpu.VMEM((all_frames, cols, ch), jnp.bfloat16),
                pltpu.VMEM((all_frames, cols, ch), jnp.bfloat16),
                pltpu.VMEM((rows, 3 * ch), jnp.float32),
                pltpu.VMEM((1, ch), jnp.float32),
                pltpu.VMEM((1, ch), jnp.float32),
                dma((3, 3, 3)),
                dma((3,)),
                dma((per_block,)),
                dma((items,)),
                dma((items,)),
                dma((items, 2)),
                dma((items, 2)),
                dma((per_block,)),
            ],
            compiler_params=pltpu.CompilerParams(
                collective_id=0, has_side_effects=True, vmem_limit_bytes=60 * 2**20
            ),
            cost_estimate=pl.CostEstimate(
                flops=2 * all_frames * cols * 27 * ch * ch,
                bytes_accessed=27 * ch * ch * 2,
                transcendentals=all_frames * cols * ch,
            ),
        )(latents.reshape(frames, cols, ch), conv_weight[0], gain, bias)
        return out.reshape(latents.shape)

    in_specs = (
        P("section", None, "rows", None, None),
        P("section", None, None, None, None, None),
        P("section", None),
        P("section", None),
    )
    out_specs = P("section", None, "rows", None, None)
    return jax.shard_map(body, mesh=mesh, in_specs=in_specs, out_specs=out_specs, check_vma=False)
```

```python
import functools

import jax
import jax.numpy as jnp
from jax import lax
from jax.experimental import pallas as pl
from jax.experimental.pallas import tpu as pltpu
from jax.sharding import PartitionSpec as P

EPSILON = 1e-06
GROUP = 2


def kernel(
    sections, row_count, group,
    lat_ref, w_hbm, gain_hbm, bias_hbm, o_ref,
    weights, acts, incoming, outgoing, total, gain_ref, bias_ref,
    w_sem, small_sem, lat_send, in_recv, out_send, halo_send, halo_recv, own_recv,
):
    frames, cols, ch = lat_ref.shape
    all_frames = sections * frames
    per_block = frames // group
    items = sections * per_block
    rows = group * cols
    section = lax.axis_index("section")
    row = lax.axis_index("rows")
    last = sections - 1

    barrier = pltpu.get_barrier_semaphore()
    for peer in range(sections):
        copies_here = (
            (peer == section - 1)
            | ((section == 0) & (peer > 0))
            | ((peer == last) & (section < last))
        )

        @pl.when(copies_here)
        def _():
            pl.semaphore_signal(barrier, inc=1, device_id={"section": peer})

    @pl.when(row > 0)
    def _():
        pl.semaphore_signal(barrier, inc=1, device_id={"rows": row - 1})

    @pl.when(row < row_count - 1)
    def _():
        pl.semaphore_signal(barrier, inc=1, device_id={"rows": row + 1})

    place = {
        (1, 0): 0, (1, 2): 1, (2, 0): 2, (2, 2): 3,
        (1, 1): 4, (2, 1): 5,
        (0, 0): 6, (0, 2): 7, (0, 1): 8,
    }
    own_taps = ((1, 1), (2, 1))
    halo_taps = ((1, 0), (1, 2), (2, 0), (2, 2))
    old_taps = ((0, 0), (0, 2), (0, 1))

    def weight_copy(i, j, k):
        return pltpu.make_async_copy(
            w_hbm.at[i, j, k],
            weights.at[pl.ds(place[i, j] * ch, ch), pl.ds(k * ch, ch)],
            w_sem.at[i, j, k],
        )

    def weights_start(taps):
        for i, j in taps:
            for k in range(3):
                weight_copy(i, j, k).start(priority=1)

    def weights_here(taps):
        for i, j in taps:
            for k in range(3):
                weight_copy(i, j, k).wait()

    gain_copy = pltpu.make_async_copy(gain_hbm, gain_ref, small_sem.at[0])
    bias_copy = pltpu.make_async_copy(bias_hbm, bias_ref, small_sem.at[1])
    first_copy = pltpu.make_async_copy(
        lat_ref, incoming.at[pl.ds(0, frames)], small_sem.at[2]
    )

    @pl.when(section == 0)
    def _():
        first_copy.start()

    gain_copy.start()
    bias_copy.start()
    weights_start(own_taps)

    @pl.when(section > 0)
    def _():
        weights_start(halo_taps + old_taps)


    acts[:, 0:2] = jnp.zeros((3, 2, cols, ch), jnp.bfloat16)

    @pl.when(row == 0)
    def _():
        acts[0] = jnp.zeros((all_frames + 2, cols, ch), jnp.bfloat16)

    @pl.when(row == row_count - 1)
    def _():
        acts[1] = jnp.zeros((all_frames + 2, cols, ch), jnp.bfloat16)

    greeted = (
        jnp.where(
            section == last, last, jnp.where(section > 0, 2, 1)
        )
        + jnp.where(row > 0, 1, 0)
        + jnp.where(row < row_count - 1, 1, 0)
    )

    def lat_copy(part):
        return pltpu.make_async_remote_copy(
            lat_ref.at[part],
            incoming.at[section * frames + part],
            lat_send.at[part],
            in_recv.at[section * frames + part],
            device_id={"section": 0},
        )

    @pl.when(section > 0)
    def _():
        pl.semaphore_wait(barrier, greeted)
        for part in range(frames):
            lat_copy(part).start()

    def pass_copy(t):
        return pltpu.make_async_remote_copy(
            outgoing.at[t],
            incoming.at[t],
            out_send.at[t],
            in_recv.at[t],
            device_id={"section": lax.rem(section + 1, sections)},
        )

    def home_copy(t):
        part = lax.rem(t, frames)
        return pltpu.make_async_remote_copy(
            outgoing.at[t],
            o_ref.at[part],
            out_send.at[t],
            own_recv.at[part],
            device_id={"section": t // frames},
        )

    def halo_copy(t, way):
        lane = 1 if way == 0 else 0
        target = row - 1 if way == 0 else row + 1
        return pltpu.make_async_remote_copy(
            acts.at[2, t + 2],
            acts.at[lane, t + 2],
            halo_send.at[t, way],
            halo_recv.at[t, way],
            device_id={"rows": target},
        )

    def product(starts, places, top):
        parts = [
            acts[at, pl.ds(start, group)].reshape(rows, ch)
            for start in starts
            for at in places
        ]
        lhs = jnp.concatenate(parts, axis=-1)
        rhs = weights[top * ch : top * ch + lhs.shape[1], :]
        return jnp.dot(lhs, rhs, preferred_element_type=jnp.float32)

    gain_copy.wait()
    bias_copy.wait()
    gain_row = gain_ref[...]
    bias_row = bias_ref[...]

    @pl.when(section == 0)
    def _():
        first_copy.wait()

    col_id = lax.broadcasted_iota(jnp.int32, (cols, ch), 0)

    def step(item, carry):
        t0 = item * group

        for part in range(group):
            t = t0 + part

            @pl.when((section > 0) | (item >= per_block))
            def _():
                pass_copy(t).wait_recv()

            x = incoming[t].astype(jnp.float32)
            mean_square = jnp.mean(x * x, axis=-1, keepdims=True)
            v = x * lax.rsqrt(mean_square + EPSILON) * gain_row
            acts[2, t + 2] = (v * jax.nn.sigmoid(v)).astype(jnp.bfloat16)

            if part == 0:
                @pl.when((section == 0) & (item == 0))
                def _():
                    pl.semaphore_wait(barrier, greeted)

            @pl.when(row > 0)
            def _():
                halo_copy(t, 0).start()

            @pl.when(row < row_count - 1)
            def _():
                halo_copy(t, 1).start()

        @pl.when((item == 0) & (section == 0))
        def _():
            weights_start(halo_taps)

        @pl.when(item == 0)
        def _():
            weights_here(own_taps)

        @pl.when(item == 1)
        def _():
            weights_here(old_taps)

        own = product((t0 + 1, t0 + 2), (2,), 4)

        @pl.when(item == 0)
        def _():
            total[...] = own
            weights_here(halo_taps)

        @pl.when(item > 0)
        def _():
            total[...] = own + product((t0,), (0, 1, 2), 6)

        for part in range(group):
            @pl.when(row < row_count - 1)
            def _():
                halo_copy(t0 + part, 0).wait_recv()

            @pl.when(row > 0)
            def _():
                halo_copy(t0 + part, 1).wait_recv()

        summed = total[...] + product((t0 + 1, t0 + 2), (0, 1), 0)
        home = (section == last) & (item >= last * per_block)
        for part in range(group):
            t = t0 + part
            here = summed[part * cols : (part + 1) * cols]
            left = pltpu.roll(here[:, 0:ch], 1, 0)
            left = jnp.where(col_id == 0, 0.0, left)
            right = pltpu.roll(here[:, 2 * ch : 3 * ch], cols - 1, 0)
            right = jnp.where(col_id == cols - 1, 0.0, right)
            x = incoming[t].astype(jnp.float32)
            y = x + (left + here[:, ch : 2 * ch] + right) + bias_row
            y = y.astype(jnp.bfloat16)

            @pl.when(home)
            def _():
                o_ref[t - last * frames] = y

            @pl.when(jnp.logical_not(home))
            def _():
                outgoing[t] = y

            @pl.when(section < last)
            def _():
                pass_copy(t).start()

            @pl.when((section == last) & (item < last * per_block))
            def _():
                home_copy(t).start()

        @pl.when((item == 0) & (section == 0))
        def _():
            weights_start(old_taps)

        return carry

    lax.fori_loop(0, items, step, 0)

    @pl.when(section > 0)
    def _():
        for part in range(frames):
            lat_copy(part).wait_send()

    def finish(t, carry):
        @pl.when(row > 0)
        def _():
            halo_copy(t, 0).wait_send()

        @pl.when(row < row_count - 1)
        def _():
            halo_copy(t, 1).wait_send()

        @pl.when((section < last) | (t < last * frames))
        def _():
            pass_copy(t).wait_send()

        return carry

    lax.fori_loop(0, all_frames, finish, 0)

    @pl.when(section < last)
    def _():
        for part in range(frames):
            home_copy(part).wait_recv()


def solution(mesh):
    sections = mesh.shape["section"]
    row_count = mesh.shape["rows"]

    def body(latents, conv_weight, gain, bias):
        _, frames, _, cols, ch = latents.shape
        group = GROUP
        all_frames = sections * frames
        rows = group * cols
        dma = pltpu.SemaphoreType.DMA
        vmem = pl.BlockSpec(memory_space=pltpu.VMEM)
        out = pl.pallas_call(
            functools.partial(kernel, sections, row_count, group),
            out_shape=jax.ShapeDtypeStruct((frames, cols, ch), jnp.bfloat16),
            in_specs=[pl.BlockSpec(memory_space=pl.ANY)] * 4,
            out_specs=vmem,
            scratch_shapes=[
                pltpu.VMEM((9 * ch, 3 * ch), jnp.bfloat16),
                pltpu.VMEM((3, all_frames + 2, cols, ch), jnp.bfloat16),
                pltpu.VMEM((all_frames, cols, ch), jnp.bfloat16),
                pltpu.VMEM((all_frames, cols, ch), jnp.bfloat16),
                pltpu.VMEM((rows, 3 * ch), jnp.float32),
                pltpu.VMEM((1, ch), jnp.float32),
                pltpu.VMEM((1, ch), jnp.float32),
                dma((3, 3, 3)),
                dma((3,)),
                dma((frames,)),
                dma((all_frames,)),
                dma((all_frames,)),
                dma((all_frames, 2)),
                dma((all_frames, 2)),
                dma((frames,)),
            ],
            compiler_params=pltpu.CompilerParams(
                collective_id=0, has_side_effects=True, vmem_limit_bytes=60 * 2**20
            ),
            cost_estimate=pl.CostEstimate(
                flops=2 * all_frames * cols * 27 * ch * ch,
                bytes_accessed=27 * ch * ch * 2,
                transcendentals=all_frames * cols * ch,
            ),
        )(latents.reshape(frames, cols, ch), conv_weight[0], gain, bias)
        return out.reshape(latents.shape)

    in_specs = (
        P("section", None, "rows", None, None),
        P("section", None, None, None, None, None),
        P("section", None),
        P("section", None),
    )
    out_specs = P("section", None, "rows", None, None)
    return jax.shard_map(body, mesh=mesh, in_specs=in_specs, out_specs=out_specs, check_vma=False)
```

```python
import functools

import jax
import jax.numpy as jnp
from jax import lax
from jax.experimental import pallas as pl
from jax.experimental.pallas import tpu as pltpu
from jax.sharding import PartitionSpec as P

EPSILON = 1e-06
GROUP = 2


def kernel(
    sections, row_count, group,
    lat_ref, w_hbm, gain_hbm, bias_hbm, o_ref,
    weights, acts, incoming, outgoing, total, gain_ref, bias_ref,
    w_sem, small_sem, lat_send, in_recv, out_send, halo_send, halo_recv, own_recv,
):
    frames, cols, ch = lat_ref.shape
    all_frames = sections * frames
    per_block = frames // group
    items = sections * per_block
    rows = group * cols
    section = lax.axis_index("section")
    row = lax.axis_index("rows")
    last = sections - 1

    barrier = pltpu.get_barrier_semaphore()
    for peer in range(sections):
        copies_here = (
            (peer == section - 1)
            | ((section == 0) & (peer > 0))
            | ((peer == last) & (section < last))
        )

        @pl.when(copies_here)
        def _():
            pl.semaphore_signal(barrier, inc=1, device_id={"section": peer})

    @pl.when(row > 0)
    def _():
        pl.semaphore_signal(barrier, inc=1, device_id={"rows": row - 1})

    @pl.when(row < row_count - 1)
    def _():
        pl.semaphore_signal(barrier, inc=1, device_id={"rows": row + 1})

    place = {
        (1, 0): 0, (1, 2): 1, (2, 0): 2, (2, 2): 3,
        (1, 1): 4, (2, 1): 5,
        (0, 0): 6, (0, 2): 7, (0, 1): 8,
    }
    own_taps = ((1, 1), (2, 1))
    halo_taps = ((1, 0), (1, 2), (2, 0), (2, 2))
    old_taps = ((0, 0), (0, 2), (0, 1))

    def weight_copy(i, j, k):
        return pltpu.make_async_copy(
            w_hbm.at[i, j, k],
            weights.at[pl.ds(place[i, j] * ch, ch), pl.ds(k * ch, ch)],
            w_sem.at[i, j, k],
        )

    def weights_start(taps):
        for i, j in taps:
            for k in range(3):
                weight_copy(i, j, k).start(priority=1)

    def weights_here(taps):
        for i, j in taps:
            for k in range(3):
                weight_copy(i, j, k).wait()

    gain_copy = pltpu.make_async_copy(gain_hbm, gain_ref, small_sem.at[0])
    bias_copy = pltpu.make_async_copy(bias_hbm, bias_ref, small_sem.at[1])
    first_copy = pltpu.make_async_copy(
        lat_ref, incoming.at[pl.ds(0, frames)], small_sem.at[2]
    )

    @pl.when(section == 0)
    def _():
        first_copy.start()

    gain_copy.start()
    bias_copy.start()
    weights_start(own_taps + halo_taps + old_taps)

    acts[:, 0:2] = jnp.zeros((3, 2, cols, ch), jnp.bfloat16)

    @pl.when(row == 0)
    def _():
        acts[0] = jnp.zeros((all_frames + 2, cols, ch), jnp.bfloat16)

    @pl.when(row == row_count - 1)
    def _():
        acts[1] = jnp.zeros((all_frames + 2, cols, ch), jnp.bfloat16)

    greeted = (
        jnp.where(
            section == last, last, jnp.where(section > 0, 2, 1)
        )
        + jnp.where(row > 0, 1, 0)
        + jnp.where(row < row_count - 1, 1, 0)
    )

    def lat_copy(part):
        return pltpu.make_async_remote_copy(
            lat_ref.at[part],
            incoming.at[section * frames + part],
            lat_send.at[part],
            in_recv.at[section * frames + part],
            device_id={"section": 0},
        )

    @pl.when(section > 0)
    def _():
        pl.semaphore_wait(barrier, greeted)
        for part in range(frames):
            lat_copy(part).start()

    def pass_copy(t):
        return pltpu.make_async_remote_copy(
            outgoing.at[t],
            incoming.at[t],
            out_send.at[t],
            in_recv.at[t],
            device_id={"section": lax.rem(section + 1, sections)},
        )

    def home_copy(t):
        part = lax.rem(t, frames)
        return pltpu.make_async_remote_copy(
            outgoing.at[t],
            o_ref.at[part],
            out_send.at[t],
            own_recv.at[part],
            device_id={"section": t // frames},
        )

    def halo_copy(t, way):
        lane = 1 if way == 0 else 0
        target = row - 1 if way == 0 else row + 1
        return pltpu.make_async_remote_copy(
            acts.at[2, t + 2],
            acts.at[lane, t + 2],
            halo_send.at[t, way],
            halo_recv.at[t, way],
            device_id={"rows": target},
        )

    def product(pieces, top):
        lhs = jnp.concatenate(
            [acts[at, pl.ds(start, group)].reshape(rows, ch) for at, start in pieces],
            axis=-1,
        )
        rhs = weights[top * ch : (top + len(pieces)) * ch, :]
        return jnp.dot(lhs, rhs, preferred_element_type=jnp.float32)

    gain_copy.wait()
    bias_copy.wait()
    gain_row = gain_ref[...]
    bias_row = bias_ref[...]

    @pl.when(section == 0)
    def _():
        first_copy.wait()

    col_id = lax.broadcasted_iota(jnp.int32, (cols, ch), 0)

    def step(item, carry):
        t0 = item * group

        for part in range(group):
            t = t0 + part

            @pl.when((section > 0) | (item >= per_block))
            def _():
                pass_copy(t).wait_recv()

            x = incoming[t].astype(jnp.float32)
            mean_square = jnp.mean(x * x, axis=-1, keepdims=True)
            v = x * lax.rsqrt(mean_square + EPSILON) * gain_row
            acts[2, t + 2] = (v * jax.nn.sigmoid(v)).astype(jnp.bfloat16)

            if part == 0:
                @pl.when((section == 0) & (item == 0))
                def _():
                    pl.semaphore_wait(barrier, greeted)

            @pl.when(row > 0)
            def _():
                halo_copy(t, 0).start()

            @pl.when(row < row_count - 1)
            def _():
                halo_copy(t, 1).start()

        own = ((2, t0 + 1), (2, t0 + 2))
        old = ((0, t0), (1, t0), (2, t0))
        halo = ((0, t0 + 1), (1, t0 + 1), (0, t0 + 2), (1, t0 + 2))

        @pl.when(item == 0)
        def _():
            weights_here(own_taps)
            total[...] = product(own, 4)
            weights_here(halo_taps)

        @pl.when(item == 1)
        def _():
            weights_here(old_taps)

        @pl.when(item > 0)
        def _():
            total[...] = product(own + old, 4)

        for part in range(group):
            @pl.when(row < row_count - 1)
            def _():
                halo_copy(t0 + part, 0).wait_recv()

            @pl.when(row > 0)
            def _():
                halo_copy(t0 + part, 1).wait_recv()

        summed = total[...] + product(halo, 0)
        home = (section == last) & (item >= last * per_block)
        for part in range(group):
            t = t0 + part
            here = summed[part * cols : (part + 1) * cols]
            left = pltpu.roll(here[:, 0:ch], 1, 0)
            left = jnp.where(col_id == 0, 0.0, left)
            right = pltpu.roll(here[:, 2 * ch : 3 * ch], cols - 1, 0)
            right = jnp.where(col_id == cols - 1, 0.0, right)
            x = incoming[t].astype(jnp.float32)
            y = x + (left + here[:, ch : 2 * ch] + right) + bias_row
            y = y.astype(jnp.bfloat16)

            @pl.when(home)
            def _():
                o_ref[t - last * frames] = y

            @pl.when(jnp.logical_not(home))
            def _():
                outgoing[t] = y

            @pl.when(section < last)
            def _():
                pass_copy(t).start()

            @pl.when((section == last) & (item < last * per_block))
            def _():
                home_copy(t).start()

        return carry

    lax.fori_loop(0, items, step, 0)

    @pl.when(section > 0)
    def _():
        for part in range(frames):
            lat_copy(part).wait_send()

    def finish(t, carry):
        @pl.when(row > 0)
        def _():
            halo_copy(t, 0).wait_send()

        @pl.when(row < row_count - 1)
        def _():
            halo_copy(t, 1).wait_send()

        @pl.when((section < last) | (t < last * frames))
        def _():
            pass_copy(t).wait_send()

        return carry

    lax.fori_loop(0, all_frames, finish, 0)

    @pl.when(section < last)
    def _():
        for part in range(frames):
            home_copy(part).wait_recv()


def solution(mesh):
    sections = mesh.shape["section"]
    row_count = mesh.shape["rows"]

    def body(latents, conv_weight, gain, bias):
        _, frames, _, cols, ch = latents.shape
        group = GROUP
        all_frames = sections * frames
        rows = group * cols
        dma = pltpu.SemaphoreType.DMA
        vmem = pl.BlockSpec(memory_space=pltpu.VMEM)
        out = pl.pallas_call(
            functools.partial(kernel, sections, row_count, group),
            out_shape=jax.ShapeDtypeStruct((frames, cols, ch), jnp.bfloat16),
            in_specs=[pl.BlockSpec(memory_space=pl.ANY)] * 4,
            out_specs=vmem,
            scratch_shapes=[
                pltpu.VMEM((9 * ch, 3 * ch), jnp.bfloat16),
                pltpu.VMEM((3, all_frames + 2, cols, ch), jnp.bfloat16),
                pltpu.VMEM((all_frames, cols, ch), jnp.bfloat16),
                pltpu.VMEM((all_frames, cols, ch), jnp.bfloat16),
                pltpu.VMEM((rows, 3 * ch), jnp.float32),
                pltpu.VMEM((1, ch), jnp.float32),
                pltpu.VMEM((1, ch), jnp.float32),
                dma((3, 3, 3)),
                dma((3,)),
                dma((frames,)),
                dma((all_frames,)),
                dma((all_frames,)),
                dma((all_frames, 2)),
                dma((all_frames, 2)),
                dma((frames,)),
            ],
            compiler_params=pltpu.CompilerParams(
                collective_id=0, has_side_effects=True, vmem_limit_bytes=60 * 2**20
            ),
            cost_estimate=pl.CostEstimate(
                flops=2 * all_frames * cols * 27 * ch * ch,
                bytes_accessed=27 * ch * ch * 2,
                transcendentals=all_frames * cols * ch,
            ),
        )(latents.reshape(frames, cols, ch), conv_weight[0], gain, bias)
        return out.reshape(latents.shape)

    in_specs = (
        P("section", None, "rows", None, None),
        P("section", None, None, None, None, None),
        P("section", None),
        P("section", None),
    )
    out_specs = P("section", None, "rows", None, None)
    return jax.shard_map(body, mesh=mesh, in_specs=in_specs, out_specs=out_specs, check_vma=False)
```

```python
import functools

import jax
import jax.numpy as jnp
from jax import lax
from jax.experimental import pallas as pl
from jax.experimental.pallas import tpu as pltpu
from jax.sharding import PartitionSpec as P

EPSILON = 1e-06
GROUP = 2


def kernel(
    sections, row_count, group,
    lat_ref, w_hbm, gain_hbm, bias_hbm, o_ref,
    weights, acts, incoming, outgoing, total, gain_ref, bias_ref,
    w_sem, small_sem, lat_send, in_recv, out_send, halo_send, halo_recv, own_recv,
):
    frames, cols, ch = lat_ref.shape
    all_frames = sections * frames
    per_block = frames // group
    items = sections * per_block
    rows = group * cols
    section = lax.axis_index("section")
    row = lax.axis_index("rows")
    last = sections - 1

    barrier = pltpu.get_barrier_semaphore()
    for peer in range(sections):
        copies_here = (
            (peer == section - 1)
            | ((section == 0) & (peer > 0))
            | ((peer == last) & (section < last))
        )

        @pl.when(copies_here)
        def _():
            pl.semaphore_signal(barrier, inc=1, device_id={"section": peer})

    @pl.when(row > 0)
    def _():
        pl.semaphore_signal(barrier, inc=1, device_id={"rows": row - 1})

    @pl.when(row < row_count - 1)
    def _():
        pl.semaphore_signal(barrier, inc=1, device_id={"rows": row + 1})

    place = {
        (1, 0): 0, (1, 2): 1, (2, 0): 2, (2, 2): 3,
        (1, 1): 4, (2, 1): 5,
        (0, 0): 6, (0, 2): 7, (0, 1): 8,
    }
    own_taps = ((1, 1), (2, 1))
    halo_taps = ((1, 0), (1, 2), (2, 0), (2, 2))
    old_taps = ((0, 0), (0, 2), (0, 1))

    def weight_copy(i, j, k):
        return pltpu.make_async_copy(
            w_hbm.at[i, j, k],
            weights.at[pl.ds(place[i, j] * ch, ch), pl.ds(k * ch, ch)],
            w_sem.at[i, j, k],
        )

    def weights_start(taps):
        for i, j in taps:
            for k in range(3):
                weight_copy(i, j, k).start(priority=1)

    def weights_here(taps):
        for i, j in taps:
            for k in range(3):
                weight_copy(i, j, k).wait()

    gain_copy = pltpu.make_async_copy(gain_hbm, gain_ref, small_sem.at[0])
    bias_copy = pltpu.make_async_copy(bias_hbm, bias_ref, small_sem.at[1])
    first_copy = pltpu.make_async_copy(
        lat_ref, incoming.at[pl.ds(0, frames)], small_sem.at[2]
    )

    @pl.when(section == 0)
    def _():
        first_copy.start()

    gain_copy.start()
    bias_copy.start()
    weights_start(own_taps + halo_taps + old_taps)

    acts[:, 0:2] = jnp.zeros((3, 2, cols, ch), jnp.bfloat16)

    @pl.when(row == 0)
    def _():
        acts[0] = jnp.zeros((all_frames + 2, cols, ch), jnp.bfloat16)

    @pl.when(row == row_count - 1)
    def _():
        acts[1] = jnp.zeros((all_frames + 2, cols, ch), jnp.bfloat16)

    greeted = (
        jnp.where(
            section == last, last, jnp.where(section > 0, 2, 1)
        )
        + jnp.where(row > 0, 1, 0)
        + jnp.where(row < row_count - 1, 1, 0)
    )

    def lat_copy(part):
        return pltpu.make_async_remote_copy(
            lat_ref.at[part],
            incoming.at[section * frames + part],
            lat_send.at[part],
            in_recv.at[section * frames + part],
            device_id={"section": 0},
        )

    @pl.when(section >= 2)
    def _():
        weights_here(own_taps + halo_taps + old_taps)

    @pl.when(section > 0)
    def _():
        pl.semaphore_wait(barrier, greeted)
        for part in range(frames):
            lat_copy(part).start()

    def pass_copy(t):
        return pltpu.make_async_remote_copy(
            outgoing.at[t],
            incoming.at[t],
            out_send.at[t],
            in_recv.at[t],
            device_id={"section": lax.rem(section + 1, sections)},
        )

    def home_copy(t):
        part = lax.rem(t, frames)
        return pltpu.make_async_remote_copy(
            outgoing.at[t],
            o_ref.at[part],
            out_send.at[t],
            own_recv.at[part],
            device_id={"section": t // frames},
        )

    def halo_copy(t, way):
        lane = 1 if way == 0 else 0
        target = row - 1 if way == 0 else row + 1
        return pltpu.make_async_remote_copy(
            acts.at[2, t + 2],
            acts.at[lane, t + 2],
            halo_send.at[t, way],
            halo_recv.at[t, way],
            device_id={"rows": target},
        )

    def product(pieces, top, add):
        lhs = jnp.concatenate(
            [acts[at, pl.ds(start, group)].reshape(rows, ch) for at, start in pieces],
            axis=-1,
        )
        for low in range(0, 3 * ch, 256):
            high = min(low + 256, 3 * ch)
            part = jnp.dot(
                lhs,
                weights[top * ch : (top + len(pieces)) * ch, low:high],
                preferred_element_type=jnp.float32,
            )
            if add:
                part += total[:, low:high]
            total[:, low:high] = part

    gain_copy.wait()
    bias_copy.wait()
    gain_row = gain_ref[...]
    bias_row = bias_ref[...]

    @pl.when(section == 0)
    def _():
        first_copy.wait()

    col_id = lax.broadcasted_iota(jnp.int32, (cols, ch), 0)

    def step(item, carry):
        t0 = item * group

        for part in range(group):
            t = t0 + part

            @pl.when((section > 0) | (item >= per_block))
            def _():
                pass_copy(t).wait_recv()

            x = incoming[t].astype(jnp.float32)
            mean_square = jnp.mean(x * x, axis=-1, keepdims=True)
            v = x * lax.rsqrt(mean_square + EPSILON) * gain_row
            acts[2, t + 2] = (v * jax.nn.sigmoid(v)).astype(jnp.bfloat16)

            if part == 0:
                @pl.when((section == 0) & (item == 0))
                def _():
                    pl.semaphore_wait(barrier, greeted)

            @pl.when(row > 0)
            def _():
                halo_copy(t, 0).start()

            @pl.when(row < row_count - 1)
            def _():
                halo_copy(t, 1).start()

        own = ((2, t0 + 1), (2, t0 + 2))
        old = ((0, t0), (1, t0), (2, t0))
        halo = ((0, t0 + 1), (1, t0 + 1), (0, t0 + 2), (1, t0 + 2))

        @pl.when((item == 0) & (section < 2))
        def _():
            weights_here(own_taps)

        @pl.when(item == 0)
        def _():
            product(own, 4, False)

        @pl.when((item == 0) & (section < 2))
        def _():
            weights_here(halo_taps)

        @pl.when((item == 1) & (section < 2))
        def _():
            weights_here(old_taps)

        @pl.when(item > 0)
        def _():
            product(own + old, 4, False)

        for part in range(group):
            @pl.when(row < row_count - 1)
            def _():
                halo_copy(t0 + part, 0).wait_recv()

            @pl.when(row > 0)
            def _():
                halo_copy(t0 + part, 1).wait_recv()

        product(halo, 0, True)
        home = (section == last) & (item >= last * per_block)
        for part in range(group):
            t = t0 + part
            here = total[part * cols : (part + 1) * cols, :]
            left = pltpu.roll(here[:, 0:ch], 1, 0)
            left = jnp.where(col_id == 0, 0.0, left)
            right = pltpu.roll(here[:, 2 * ch : 3 * ch], cols - 1, 0)
            right = jnp.where(col_id == cols - 1, 0.0, right)
            x = incoming[t].astype(jnp.float32)
            y = x + (left + here[:, ch : 2 * ch] + right) + bias_row
            y = y.astype(jnp.bfloat16)

            @pl.when(home)
            def _():
                o_ref[t - last * frames] = y

            @pl.when(jnp.logical_not(home))
            def _():
                outgoing[t] = y

            @pl.when(section < last)
            def _():
                pass_copy(t).start()

            @pl.when((section == last) & (item < last * per_block))
            def _():
                home_copy(t).start()

        return carry

    lax.fori_loop(0, items, step, 0)

    @pl.when(section > 0)
    def _():
        for part in range(frames):
            lat_copy(part).wait_send()

    def finish(t, carry):
        @pl.when(row > 0)
        def _():
            halo_copy(t, 0).wait_send()

        @pl.when(row < row_count - 1)
        def _():
            halo_copy(t, 1).wait_send()

        @pl.when((section < last) | (t < last * frames))
        def _():
            pass_copy(t).wait_send()

        return carry

    lax.fori_loop(0, all_frames, finish, 0)

    @pl.when(section < last)
    def _():
        for part in range(frames):
            home_copy(part).wait_recv()


def solution(mesh):
    sections = mesh.shape["section"]
    row_count = mesh.shape["rows"]

    def body(latents, conv_weight, gain, bias):
        _, frames, _, cols, ch = latents.shape
        group = GROUP
        all_frames = sections * frames
        rows = group * cols
        dma = pltpu.SemaphoreType.DMA
        vmem = pl.BlockSpec(memory_space=pltpu.VMEM)
        out = pl.pallas_call(
            functools.partial(kernel, sections, row_count, group),
            out_shape=jax.ShapeDtypeStruct((frames, cols, ch), jnp.bfloat16),
            in_specs=[pl.BlockSpec(memory_space=pl.ANY)] * 4,
            out_specs=vmem,
            scratch_shapes=[
                pltpu.VMEM((9 * ch, 3 * ch), jnp.bfloat16),
                pltpu.VMEM((3, all_frames + 2, cols, ch), jnp.bfloat16),
                pltpu.VMEM((all_frames, cols, ch), jnp.bfloat16),
                pltpu.VMEM((all_frames, cols, ch), jnp.bfloat16),
                pltpu.VMEM((rows, 3 * ch), jnp.float32),
                pltpu.VMEM((1, ch), jnp.float32),
                pltpu.VMEM((1, ch), jnp.float32),
                dma((3, 3, 3)),
                dma((3,)),
                dma((frames,)),
                dma((all_frames,)),
                dma((all_frames,)),
                dma((all_frames, 2)),
                dma((all_frames, 2)),
                dma((frames,)),
            ],
            compiler_params=pltpu.CompilerParams(
                collective_id=0, has_side_effects=True, vmem_limit_bytes=60 * 2**20
            ),
            cost_estimate=pl.CostEstimate(
                flops=2 * all_frames * cols * 27 * ch * ch,
                bytes_accessed=27 * ch * ch * 2,
                transcendentals=all_frames * cols * ch,
            ),
        )(latents.reshape(frames, cols, ch), conv_weight[0], gain, bias)
        return out.reshape(latents.shape)

    in_specs = (
        P("section", None, "rows", None, None),
        P("section", None, None, None, None, None),
        P("section", None),
        P("section", None),
    )
    out_specs = P("section", None, "rows", None, None)
    return jax.shard_map(body, mesh=mesh, in_specs=in_specs, out_specs=out_specs, check_vma=False)
```

```python
import functools

import jax
import jax.numpy as jnp
from jax import lax
from jax.experimental import pallas as pl
from jax.experimental.pallas import tpu as pltpu
from jax.sharding import PartitionSpec as P

EPSILON = 1e-06
GROUP = 2


def kernel(
    sections, row_count, group,
    lat_ref, w_hbm, gain_hbm, bias_hbm, o_ref,
    weights, acts, incoming, outgoing, total, gain_ref, bias_ref,
    w_sem, small_sem, lat_send, in_recv, out_send, halo_send, halo_recv, own_recv,
):
    frames, cols, ch = lat_ref.shape
    all_frames = sections * frames
    per_block = frames // group
    items = sections * per_block
    rows = group * cols
    section = lax.axis_index("section")
    row = lax.axis_index("rows")
    last = sections - 1

    barrier = pltpu.get_barrier_semaphore()
    for peer in range(sections):
        copies_here = (
            (peer == section - 1)
            | ((section == 0) & (peer > 0))
            | ((peer == last) & (section < last))
        )

        @pl.when(copies_here)
        def _():
            pl.semaphore_signal(barrier, inc=1, device_id={"section": peer})

    @pl.when(row > 0)
    def _():
        pl.semaphore_signal(barrier, inc=1, device_id={"rows": row - 1})

    @pl.when(row < row_count - 1)
    def _():
        pl.semaphore_signal(barrier, inc=1, device_id={"rows": row + 1})

    place = {
        (1, 0): 0, (1, 2): 1, (2, 0): 2, (2, 2): 3,
        (1, 1): 4, (2, 1): 5,
        (0, 0): 6, (0, 2): 7, (0, 1): 8,
    }
    own_taps = ((1, 1), (2, 1))
    halo_taps = ((1, 0), (1, 2), (2, 0), (2, 2))
    old_taps = ((0, 0), (0, 2), (0, 1))

    def weight_copy(i, j, k):
        return pltpu.make_async_copy(
            w_hbm.at[i, j, k],
            weights.at[pl.ds(place[i, j] * ch, ch), pl.ds(k * ch, ch)],
            w_sem.at[i, j, k],
        )

    def weights_start(taps):
        for i, j in taps:
            for k in range(3):
                weight_copy(i, j, k).start(priority=1)

    def weights_here(taps):
        for i, j in taps:
            for k in range(3):
                weight_copy(i, j, k).wait()

    gain_copy = pltpu.make_async_copy(gain_hbm, gain_ref, small_sem.at[0])
    bias_copy = pltpu.make_async_copy(bias_hbm, bias_ref, small_sem.at[1])
    first_copy = pltpu.make_async_copy(
        lat_ref, incoming.at[pl.ds(0, frames)], small_sem.at[2]
    )

    @pl.when(section == 0)
    def _():
        first_copy.start()

    gain_copy.start()
    bias_copy.start()
    weights_start(own_taps + halo_taps + old_taps)

    acts[:, 0:2] = jnp.zeros((3, 2, cols, ch), jnp.bfloat16)

    @pl.when(row == 0)
    def _():
        acts[0] = jnp.zeros((all_frames + 2, cols, ch), jnp.bfloat16)

    @pl.when(row == row_count - 1)
    def _():
        acts[1] = jnp.zeros((all_frames + 2, cols, ch), jnp.bfloat16)

    greeted = (
        jnp.where(
            section == last, last, jnp.where(section > 0, 2, 1)
        )
        + jnp.where(row > 0, 1, 0)
        + jnp.where(row < row_count - 1, 1, 0)
    )

    def lat_copy(part):
        return pltpu.make_async_remote_copy(
            lat_ref.at[part],
            incoming.at[section * frames + part],
            lat_send.at[part],
            in_recv.at[section * frames + part],
            device_id={"section": 0},
        )

    @pl.when(section >= 2)
    def _():
        weights_here(own_taps + halo_taps + old_taps)

    @pl.when(section > 0)
    def _():
        pl.semaphore_wait(barrier, greeted)
        for part in range(frames):
            lat_copy(part).start()

    def pass_copy(t):
        return pltpu.make_async_remote_copy(
            outgoing.at[t],
            incoming.at[t],
            out_send.at[t],
            in_recv.at[t],
            device_id={"section": lax.rem(section + 1, sections)},
        )

    def home_copy(t):
        part = lax.rem(t, frames)
        return pltpu.make_async_remote_copy(
            outgoing.at[t],
            o_ref.at[part],
            out_send.at[t],
            own_recv.at[part],
            device_id={"section": t // frames},
        )

    def halo_copy(t, way):
        lane = 1 if way == 0 else 0
        target = row - 1 if way == 0 else row + 1
        return pltpu.make_async_remote_copy(
            acts.at[2, t + 2],
            acts.at[lane, t + 2],
            halo_send.at[t, way],
            halo_recv.at[t, way],
            device_id={"rows": target},
        )

    def product(pieces, top, add):
        lhs = jnp.concatenate(
            [acts[at, pl.ds(start, group)].reshape(rows, ch) for at, start in pieces],
            axis=-1,
        )
        for low in range(0, 3 * ch, 256):
            high = min(low + 256, 3 * ch)
            part = jnp.dot(
                lhs,
                weights[top * ch : (top + len(pieces)) * ch, low:high],
                preferred_element_type=jnp.float32,
            )
            if add:
                part += total[:, low:high]
            total[:, low:high] = part

    gain_copy.wait()
    bias_copy.wait()
    gain_row = gain_ref[...]
    bias_row = bias_ref[...]

    @pl.when(section == 0)
    def _():
        first_copy.wait()

    col_id = lax.broadcasted_iota(jnp.int32, (cols, ch), 0)

    def step(item, carry):
        t0 = item * group

        for part in range(group):
            t = t0 + part

            @pl.when((section > 0) | (item >= per_block))
            def _():
                pass_copy(t).wait_recv()

            x = incoming[t].astype(jnp.float32)
            mean_square = jnp.mean(x * x, axis=-1, keepdims=True)
            v = x * lax.rsqrt(mean_square + EPSILON) * gain_row
            acts[2, t + 2] = (v * jax.nn.sigmoid(v)).astype(jnp.bfloat16)

            if part == 0:
                @pl.when((section == 0) & (item == 0))
                def _():
                    pl.semaphore_wait(barrier, greeted)

            @pl.when((row % 2 == 1) & (row < row_count - 1))
            def _():
                halo_copy(t, 1).start()

            @pl.when(row > 0)
            def _():
                halo_copy(t, 0).start()

            @pl.when((row % 2 == 0) & (row < row_count - 1))
            def _():
                halo_copy(t, 1).start()

        own = ((2, t0 + 1), (2, t0 + 2))
        old = ((0, t0), (1, t0), (2, t0))
        halo = ((0, t0 + 1), (1, t0 + 1), (0, t0 + 2), (1, t0 + 2))

        @pl.when((item == 0) & (section < 2))
        def _():
            weights_here(own_taps)

        @pl.when(item == 0)
        def _():
            product(own, 4, False)

        @pl.when((item == 0) & (section < 2))
        def _():
            weights_here(halo_taps)

        @pl.when((item == 1) & (section < 2))
        def _():
            weights_here(old_taps)

        @pl.when(item > 0)
        def _():
            product(own + old, 4, False)

        for part in range(group):
            @pl.when(row < row_count - 1)
            def _():
                halo_copy(t0 + part, 0).wait_recv()

            @pl.when(row > 0)
            def _():
                halo_copy(t0 + part, 1).wait_recv()

            if part == 0:
                product(halo[:2], 0, True)
            if part == group - 1:
                product(halo[2:], 2, True)

        home = (section == last) & (item >= last * per_block)
        for part in range(group):
            t = t0 + part
            here = total[part * cols : (part + 1) * cols, :]
            left = pltpu.roll(here[:, 0:ch], 1, 0)
            left = jnp.where(col_id == 0, 0.0, left)
            right = pltpu.roll(here[:, 2 * ch : 3 * ch], cols - 1, 0)
            right = jnp.where(col_id == cols - 1, 0.0, right)
            x = incoming[t].astype(jnp.float32)
            y = x + (left + here[:, ch : 2 * ch] + right) + bias_row
            y = y.astype(jnp.bfloat16)

            @pl.when(home)
            def _():
                o_ref[t - last * frames] = y

            @pl.when(jnp.logical_not(home))
            def _():
                outgoing[t] = y

            @pl.when(section < last)
            def _():
                pass_copy(t).start()

            @pl.when((section == last) & (item < last * per_block))
            def _():
                home_copy(t).start()

        return carry

    lax.fori_loop(0, items, step, 0)

    @pl.when(section > 0)
    def _():
        for part in range(frames):
            lat_copy(part).wait_send()

    def finish(t, carry):
        @pl.when(row > 0)
        def _():
            halo_copy(t, 0).wait_send()

        @pl.when(row < row_count - 1)
        def _():
            halo_copy(t, 1).wait_send()

        @pl.when((section < last) | (t < last * frames))
        def _():
            pass_copy(t).wait_send()

        return carry

    lax.fori_loop(0, all_frames, finish, 0)

    @pl.when(section < last)
    def _():
        for part in range(frames):
            home_copy(part).wait_recv()


def solution(mesh):
    sections = mesh.shape["section"]
    row_count = mesh.shape["rows"]

    def body(latents, conv_weight, gain, bias):
        _, frames, _, cols, ch = latents.shape
        group = GROUP
        all_frames = sections * frames
        rows = group * cols
        dma = pltpu.SemaphoreType.DMA
        vmem = pl.BlockSpec(memory_space=pltpu.VMEM)
        out = pl.pallas_call(
            functools.partial(kernel, sections, row_count, group),
            out_shape=jax.ShapeDtypeStruct((frames, cols, ch), jnp.bfloat16),
            in_specs=[pl.BlockSpec(memory_space=pl.ANY)] * 4,
            out_specs=vmem,
            scratch_shapes=[
                pltpu.VMEM((9 * ch, 3 * ch), jnp.bfloat16),
                pltpu.VMEM((3, all_frames + 2, cols, ch), jnp.bfloat16),
                pltpu.VMEM((all_frames, cols, ch), jnp.bfloat16),
                pltpu.VMEM((all_frames, cols, ch), jnp.bfloat16),
                pltpu.VMEM((rows, 3 * ch), jnp.float32),
                pltpu.VMEM((1, ch), jnp.float32),
                pltpu.VMEM((1, ch), jnp.float32),
                dma((3, 3, 3)),
                dma((3,)),
                dma((frames,)),
                dma((all_frames,)),
                dma((all_frames,)),
                dma((all_frames, 2)),
                dma((all_frames, 2)),
                dma((frames,)),
            ],
            compiler_params=pltpu.CompilerParams(
                collective_id=0, has_side_effects=True, vmem_limit_bytes=60 * 2**20
            ),
            cost_estimate=pl.CostEstimate(
                flops=2 * all_frames * cols * 27 * ch * ch,
                bytes_accessed=27 * ch * ch * 2,
                transcendentals=all_frames * cols * ch,
            ),
        )(latents.reshape(frames, cols, ch), conv_weight[0], gain, bias)
        return out.reshape(latents.shape)

    in_specs = (
        P("section", None, "rows", None, None),
        P("section", None, None, None, None, None),
        P("section", None),
        P("section", None),
    )
    out_specs = P("section", None, "rows", None, None)
    return jax.shard_map(body, mesh=mesh, in_specs=in_specs, out_specs=out_specs, check_vma=False)
```

```python
import functools

import jax
import jax.numpy as jnp
from jax import lax
from jax.experimental import pallas as pl
from jax.experimental.pallas import tpu as pltpu
from jax.sharding import PartitionSpec as P

EPSILON = 1e-06
GROUP = 2


def kernel(
    sections, row_count, group,
    lat_ref, w_hbm, gain_hbm, bias_hbm, o_ref,
    weights, acts, incoming, outgoing, total, gain_ref, bias_ref,
    w_sem, small_sem, lat_send, in_recv, out_send, halo_send, halo_recv, own_recv,
):
    frames, cols, ch = lat_ref.shape
    all_frames = sections * frames
    per_block = frames // group
    items = sections * per_block
    rows = group * cols
    section = lax.axis_index("section")
    row = lax.axis_index("rows")
    last = sections - 1

    barrier = pltpu.get_barrier_semaphore()
    for peer in range(sections):
        copies_here = (
            (peer == section - 1)
            | ((section == 0) & (peer > 0))
            | ((peer == last) & (section < last))
        )

        @pl.when(copies_here)
        def _():
            pl.semaphore_signal(barrier, inc=1, device_id={"section": peer})

    @pl.when(row > 0)
    def _():
        pl.semaphore_signal(barrier, inc=1, device_id={"rows": row - 1})

    @pl.when(row < row_count - 1)
    def _():
        pl.semaphore_signal(barrier, inc=1, device_id={"rows": row + 1})

    place = {
        (1, 0): 0, (1, 2): 1, (2, 0): 2, (2, 2): 3,
        (1, 1): 4, (2, 1): 5,
        (0, 0): 6, (0, 2): 7, (0, 1): 8,
    }
    own_taps = ((1, 1), (2, 1))
    halo_taps = ((1, 0), (1, 2), (2, 0), (2, 2))
    old_taps = ((0, 0), (0, 2), (0, 1))

    def weight_copy(i, j, k):
        return pltpu.make_async_copy(
            w_hbm.at[i, j, k],
            weights.at[pl.ds(place[i, j] * ch, ch), pl.ds(k * ch, ch)],
            w_sem.at[i, j, k],
        )

    def weights_start(taps):
        for i, j in taps:
            for k in range(3):
                weight_copy(i, j, k).start(priority=1)

    def weights_here(taps):
        for i, j in taps:
            for k in range(3):
                weight_copy(i, j, k).wait()

    gain_copy = pltpu.make_async_copy(gain_hbm, gain_ref, small_sem.at[0])
    bias_copy = pltpu.make_async_copy(bias_hbm, bias_ref, small_sem.at[1])
    first_copy = pltpu.make_async_copy(
        lat_ref, incoming.at[pl.ds(0, frames)], small_sem.at[2]
    )

    @pl.when(section == 0)
    def _():
        first_copy.start()

    gain_copy.start()
    bias_copy.start()
    weights_start(own_taps + halo_taps + old_taps)

    acts[:, 0:2] = jnp.zeros((3, 2, cols, ch), jnp.bfloat16)

    @pl.when(row == 0)
    def _():
        acts[0] = jnp.zeros((all_frames + 2, cols, ch), jnp.bfloat16)

    @pl.when(row == row_count - 1)
    def _():
        acts[1] = jnp.zeros((all_frames + 2, cols, ch), jnp.bfloat16)

    greeted = (
        jnp.where(
            section == last, last, jnp.where(section > 0, 2, 1)
        )
        + jnp.where(row > 0, 1, 0)
        + jnp.where(row < row_count - 1, 1, 0)
    )

    def lat_copy(part):
        return pltpu.make_async_remote_copy(
            lat_ref.at[part],
            incoming.at[section * frames + part],
            lat_send.at[part],
            in_recv.at[section * frames + part],
            device_id={"section": 0},
        )

    @pl.when(section >= 2)
    def _():
        weights_here(own_taps + halo_taps + old_taps)

    @pl.when(section > 0)
    def _():
        pl.semaphore_wait(barrier, greeted)
        for part in range(frames):
            lat_copy(part).start()

    def pass_copy(t):
        return pltpu.make_async_remote_copy(
            outgoing.at[t],
            incoming.at[t],
            out_send.at[t],
            in_recv.at[t],
            device_id={"section": lax.rem(section + 1, sections)},
        )

    def home_copy(t):
        part = lax.rem(t, frames)
        return pltpu.make_async_remote_copy(
            outgoing.at[t],
            o_ref.at[part],
            out_send.at[t],
            own_recv.at[part],
            device_id={"section": t // frames},
        )

    def halo_copy(t, way):
        lane = 1 if way == 0 else 0
        target = row - 1 if way == 0 else row + 1
        return pltpu.make_async_remote_copy(
            acts.at[2, t + 2],
            acts.at[lane, t + 2],
            halo_send.at[t, way],
            halo_recv.at[t, way],
            device_id={"rows": target},
        )

    def product(pieces, top, add):
        lhs = jnp.concatenate(
            [acts[at, pl.ds(start, group)].reshape(rows, ch) for at, start in pieces],
            axis=-1,
        )
        for low in range(0, 3 * ch, 256):
            high = min(low + 256, 3 * ch)
            part = jnp.dot(
                lhs,
                weights[top * ch : (top + len(pieces)) * ch, low:high],
                preferred_element_type=jnp.float32,
            )
            if add:
                part += total[:, low:high]
            total[:, low:high] = part

    gain_copy.wait()
    bias_copy.wait()
    gain_row = gain_ref[...]
    bias_row = bias_ref[...]

    @pl.when(section == 0)
    def _():
        first_copy.wait()

    col_id = lax.broadcasted_iota(jnp.int32, (cols, ch), 0)

    def activate(item):
        t0 = item * group
        for part in range(group):
            t = t0 + part

            @pl.when((section > 0) | (item >= per_block))
            def _():
                pass_copy(t).wait_recv()

            x = incoming[t].astype(jnp.float32)
            mean_square = jnp.mean(x * x, axis=-1, keepdims=True)
            v = x * lax.rsqrt(mean_square + EPSILON) * gain_row
            acts[2, t + 2] = (v * jax.nn.sigmoid(v)).astype(jnp.bfloat16)

            if part == 0:
                @pl.when((section == 0) & (item == 0))
                def _():
                    pl.semaphore_wait(barrier, greeted)

            @pl.when((row % 2 == 1) & (row < row_count - 1))
            def _():
                halo_copy(t, 1).start()

            @pl.when(row > 0)
            def _():
                halo_copy(t, 0).start()

            @pl.when((row % 2 == 0) & (row < row_count - 1))
            def _():
                halo_copy(t, 1).start()

    activate(jnp.int32(0))

    def step(item, carry):
        t0 = item * group

        own = ((2, t0 + 1), (2, t0 + 2))
        old = ((0, t0), (1, t0), (2, t0))
        halo = ((0, t0 + 1), (1, t0 + 1), (0, t0 + 2), (1, t0 + 2))

        @pl.when((item == 0) & (section < 2))
        def _():
            weights_here(own_taps)

        @pl.when(item == 0)
        def _():
            product(own, 4, False)

        @pl.when((item == 0) & (section < 2))
        def _():
            weights_here(halo_taps)

        @pl.when((item == 1) & (section < 2))
        def _():
            weights_here(old_taps)

        @pl.when(item > 0)
        def _():
            product(own + old, 4, False)

        @pl.when((item > 0) & (item < items - 1))
        def _():
            activate(item + 1)

        for part in range(group):
            @pl.when(row < row_count - 1)
            def _():
                halo_copy(t0 + part, 0).wait_recv()

            @pl.when(row > 0)
            def _():
                halo_copy(t0 + part, 1).wait_recv()

            if part == 0:
                product(halo[:2], 0, True)
            if part == group - 1:
                product(halo[2:], 2, True)

        home = (section == last) & (item >= last * per_block)
        for part in range(group):
            t = t0 + part
            here = total[part * cols : (part + 1) * cols, :]
            left = pltpu.roll(here[:, 0:ch], 1, 0)
            left = jnp.where(col_id == 0, 0.0, left)
            right = pltpu.roll(here[:, 2 * ch : 3 * ch], cols - 1, 0)
            right = jnp.where(col_id == cols - 1, 0.0, right)
            x = incoming[t].astype(jnp.float32)
            y = x + (left + here[:, ch : 2 * ch] + right) + bias_row
            y = y.astype(jnp.bfloat16)

            @pl.when(home)
            def _():
                o_ref[t - last * frames] = y

            @pl.when(jnp.logical_not(home))
            def _():
                outgoing[t] = y

            @pl.when(section < last)
            def _():
                pass_copy(t).start()

            @pl.when((section == last) & (item < last * per_block))
            def _():
                home_copy(t).start()

        @pl.when((item == 0) & (items > 1))
        def _():
            activate(item + 1)

        return carry

    lax.fori_loop(0, items, step, 0)

    @pl.when(section > 0)
    def _():
        for part in range(frames):
            lat_copy(part).wait_send()

    def finish(t, carry):
        @pl.when(row > 0)
        def _():
            halo_copy(t, 0).wait_send()

        @pl.when(row < row_count - 1)
        def _():
            halo_copy(t, 1).wait_send()

        @pl.when((section < last) | (t < last * frames))
        def _():
            pass_copy(t).wait_send()

        return carry

    lax.fori_loop(0, all_frames, finish, 0)

    @pl.when(section < last)
    def _():
        for part in range(frames):
            home_copy(part).wait_recv()


def solution(mesh):
    sections = mesh.shape["section"]
    row_count = mesh.shape["rows"]

    def body(latents, conv_weight, gain, bias):
        _, frames, _, cols, ch = latents.shape
        group = GROUP
        all_frames = sections * frames
        rows = group * cols
        dma = pltpu.SemaphoreType.DMA
        vmem = pl.BlockSpec(memory_space=pltpu.VMEM)
        out = pl.pallas_call(
            functools.partial(kernel, sections, row_count, group),
            out_shape=jax.ShapeDtypeStruct((frames, cols, ch), jnp.bfloat16),
            in_specs=[pl.BlockSpec(memory_space=pl.ANY)] * 4,
            out_specs=vmem,
            scratch_shapes=[
                pltpu.VMEM((9 * ch, 3 * ch), jnp.bfloat16),
                pltpu.VMEM((3, all_frames + 2, cols, ch), jnp.bfloat16),
                pltpu.VMEM((all_frames, cols, ch), jnp.bfloat16),
                pltpu.VMEM((all_frames, cols, ch), jnp.bfloat16),
                pltpu.VMEM((rows, 3 * ch), jnp.float32),
                pltpu.VMEM((1, ch), jnp.float32),
                pltpu.VMEM((1, ch), jnp.float32),
                dma((3, 3, 3)),
                dma((3,)),
                dma((frames,)),
                dma((all_frames,)),
                dma((all_frames,)),
                dma((all_frames, 2)),
                dma((all_frames, 2)),
                dma((frames,)),
            ],
            compiler_params=pltpu.CompilerParams(
                collective_id=0, has_side_effects=True, vmem_limit_bytes=60 * 2**20
            ),
            cost_estimate=pl.CostEstimate(
                flops=2 * all_frames * cols * 27 * ch * ch,
                bytes_accessed=27 * ch * ch * 2,
                transcendentals=all_frames * cols * ch,
            ),
        )(latents.reshape(frames, cols, ch), conv_weight[0], gain, bias)
        return out.reshape(latents.shape)

    in_specs = (
        P("section", None, "rows", None, None),
        P("section", None, None, None, None, None),
        P("section", None),
        P("section", None),
    )
    out_specs = P("section", None, "rows", None, None)
    return jax.shard_map(body, mesh=mesh, in_specs=in_specs, out_specs=out_specs, check_vma=False)
```

```python
import functools

import jax
import jax.numpy as jnp
from jax import lax
from jax.experimental import pallas as pl
from jax.experimental.pallas import tpu as pltpu
from jax.sharding import PartitionSpec as P

EPSILON = 1e-06
GROUP = 2


def kernel(
    sections, row_count, group,
    lat_ref, w_hbm, gain_hbm, bias_hbm, o_ref,
    weights, acts, incoming, outgoing, total, gain_ref, bias_ref,
    w_sem, small_sem, lat_send, in_recv, out_send, halo_send, halo_recv, own_recv,
):
    frames, cols, ch = lat_ref.shape
    all_frames = sections * frames
    per_block = frames // group
    items = sections * per_block
    rows = group * cols
    section = lax.axis_index("section")
    row = lax.axis_index("rows")
    last = sections - 1

    barrier = pltpu.get_barrier_semaphore()
    for peer in range(sections):
        copies_here = (
            (peer == section - 1)
            | ((section == 0) & (peer > 0))
            | ((peer == last) & (section < last))
        )

        @pl.when(copies_here)
        def _():
            pl.semaphore_signal(barrier, inc=1, device_id={"section": peer})

    @pl.when(row > 0)
    def _():
        pl.semaphore_signal(barrier, inc=1, device_id={"rows": row - 1})

    @pl.when(row < row_count - 1)
    def _():
        pl.semaphore_signal(barrier, inc=1, device_id={"rows": row + 1})

    place = {
        (1, 0): 0, (1, 2): 1, (2, 0): 2, (2, 2): 3,
        (1, 1): 4, (2, 1): 5,
        (0, 0): 6, (0, 2): 7, (0, 1): 8,
    }
    own_taps = ((1, 1), (2, 1))
    halo_taps = ((1, 0), (1, 2), (2, 0), (2, 2))
    old_taps = ((0, 0), (0, 2), (0, 1))

    def weight_copy(i, j, k):
        return pltpu.make_async_copy(
            w_hbm.at[i, j, k],
            weights.at[pl.ds(place[i, j] * ch, ch), pl.ds(k * ch, ch)],
            w_sem.at[i, j, k],
        )

    def weights_start(taps):
        for i, j in taps:
            for k in range(3):
                weight_copy(i, j, k).start(priority=1)

    def weights_here(taps):
        for i, j in taps:
            for k in range(3):
                weight_copy(i, j, k).wait()

    gain_copy = pltpu.make_async_copy(gain_hbm, gain_ref, small_sem.at[0])
    bias_copy = pltpu.make_async_copy(bias_hbm, bias_ref, small_sem.at[1])
    first_copy = pltpu.make_async_copy(
        lat_ref, incoming.at[pl.ds(0, frames)], small_sem.at[2]
    )

    @pl.when(section == 0)
    def _():
        first_copy.start()

    gain_copy.start()
    bias_copy.start()
    weights_start(own_taps + halo_taps + old_taps)

    acts[:, 0:2] = jnp.zeros((3, 2, cols, ch), jnp.bfloat16)

    @pl.when(row == 0)
    def _():
        acts[0] = jnp.zeros((all_frames + 2, cols, ch), jnp.bfloat16)

    @pl.when(row == row_count - 1)
    def _():
        acts[1] = jnp.zeros((all_frames + 2, cols, ch), jnp.bfloat16)

    greeted = (
        jnp.where(
            section == last, last, jnp.where(section > 0, 2, 1)
        )
        + jnp.where(row > 0, 1, 0)
        + jnp.where(row < row_count - 1, 1, 0)
    )

    def lat_copy(part):
        return pltpu.make_async_remote_copy(
            lat_ref.at[part],
            incoming.at[section * frames + part],
            lat_send.at[part],
            in_recv.at[section * frames + part],
            device_id={"section": 0},
        )

    @pl.when(section >= 2)
    def _():
        weights_here(own_taps + halo_taps + old_taps)

    @pl.when(section > 0)
    def _():
        pl.semaphore_wait(barrier, greeted)
        for part in range(frames):
            lat_copy(part).start()

    def pass_copy(t):
        return pltpu.make_async_remote_copy(
            outgoing.at[t],
            incoming.at[t],
            out_send.at[t],
            in_recv.at[t],
            device_id={"section": lax.rem(section + 1, sections)},
        )

    def home_copy(t):
        part = lax.rem(t, frames)
        return pltpu.make_async_remote_copy(
            outgoing.at[t],
            o_ref.at[part],
            out_send.at[t],
            own_recv.at[part],
            device_id={"section": t // frames},
        )

    def halo_copy(t, way):
        lane = 1 if way == 0 else 0
        target = row - 1 if way == 0 else row + 1
        return pltpu.make_async_remote_copy(
            acts.at[2, t + 2],
            acts.at[lane, t + 2],
            halo_send.at[t, way],
            halo_recv.at[t, way],
            device_id={"rows": target},
        )

    def product(pieces, top, add):
        lhs = jnp.concatenate(
            [acts[at, pl.ds(start, group)].reshape(rows, ch) for at, start in pieces],
            axis=-1,
        )
        for low in range(0, 3 * ch, 256):
            high = min(low + 256, 3 * ch)
            part = jnp.dot(
                lhs,
                weights[top * ch : (top + len(pieces)) * ch, low:high],
                preferred_element_type=jnp.float32,
            )
            if add:
                part += total[:, low:high]
            total[:, low:high] = part

    gain_copy.wait()
    bias_copy.wait()
    gain_row = gain_ref[...]
    bias_row = bias_ref[...]

    @pl.when(section == 0)
    def _():
        first_copy.wait()

    col_id = lax.broadcasted_iota(jnp.int32, (cols, ch), 0)

    def activate(item):
        t0 = item * group
        for part in range(group):
            t = t0 + part

            @pl.when((section > 0) | (item >= per_block))
            def _():
                pass_copy(t).wait_recv()

            x = incoming[t].astype(jnp.float32)
            mean_square = jnp.mean(x * x, axis=-1, keepdims=True)
            v = x * lax.rsqrt(mean_square + EPSILON) * gain_row
            acts[2, t + 2] = (v * jax.nn.sigmoid(v)).astype(jnp.bfloat16)

            if part == 0:
                @pl.when((section == 0) & (item == 0))
                def _():
                    pl.semaphore_wait(barrier, greeted)

            @pl.when((row % 2 == 1) & (row < row_count - 1))
            def _():
                halo_copy(t, 1).start()

            @pl.when(row > 0)
            def _():
                halo_copy(t, 0).start()

            @pl.when((row % 2 == 0) & (row < row_count - 1))
            def _():
                halo_copy(t, 1).start()

    activate(jnp.int32(0))

    def finish(t, carry):
        @pl.when(row > 0)
        def _():
            halo_copy(t, 0).wait_send()

        @pl.when(row < row_count - 1)
        def _():
            halo_copy(t, 1).wait_send()

        @pl.when((section < last) | (t < last * frames))
        def _():
            pass_copy(t).wait_send()

        return carry

    def step(item, carry):
        t0 = item * group

        own = ((2, t0 + 1), (2, t0 + 2))
        old = ((0, t0), (1, t0), (2, t0))
        halo = ((0, t0 + 1), (1, t0 + 1), (0, t0 + 2), (1, t0 + 2))

        @pl.when((item == 0) & (section < 2))
        def _():
            weights_here(own_taps)

        @pl.when(item == 0)
        def _():
            product(own, 4, False)

        @pl.when((item == 0) & (section < 2))
        def _():
            weights_here(halo_taps)

        @pl.when((item == 1) & (section < 2))
        def _():
            weights_here(old_taps)

        @pl.when(item > 0)
        def _():
            product(own + old, 4, False)

        @pl.when((item > 0) & (item < items - 1))
        def _():
            activate(item + 1)

        @pl.when(item > 0)
        def _():
            for part in range(group):
                finish(t0 - group + part, 0)

        for part in range(group):
            @pl.when(row < row_count - 1)
            def _():
                halo_copy(t0 + part, 0).wait_recv()

            @pl.when(row > 0)
            def _():
                halo_copy(t0 + part, 1).wait_recv()

            if part == 0:
                product(halo[:2], 0, True)
            if part == group - 1:
                product(halo[2:], 2, True)

        home = (section == last) & (item >= last * per_block)
        for part in range(group):
            t = t0 + part
            here = total[part * cols : (part + 1) * cols, :]
            left = pltpu.roll(here[:, 0:ch], 1, 0)
            left = jnp.where(col_id == 0, 0.0, left)
            right = pltpu.roll(here[:, 2 * ch : 3 * ch], cols - 1, 0)
            right = jnp.where(col_id == cols - 1, 0.0, right)
            x = incoming[t].astype(jnp.float32)
            y = x + (left + here[:, ch : 2 * ch] + right) + bias_row
            y = y.astype(jnp.bfloat16)

            @pl.when(home)
            def _():
                o_ref[t - last * frames] = y

            @pl.when(jnp.logical_not(home))
            def _():
                outgoing[t] = y

            @pl.when(section < last)
            def _():
                pass_copy(t).start()

            @pl.when((section == last) & (item < last * per_block))
            def _():
                home_copy(t).start()

        @pl.when((item == 0) & (items > 1))
        def _():
            activate(item + 1)

        return carry

    lax.fori_loop(0, items, step, 0)

    @pl.when(section > 0)
    def _():
        for part in range(frames):
            lat_copy(part).wait_send()

    lax.fori_loop(all_frames - group, all_frames, finish, 0)

    @pl.when(section < last)
    def _():
        for part in range(frames):
            home_copy(part).wait_recv()


def solution(mesh):
    sections = mesh.shape["section"]
    row_count = mesh.shape["rows"]

    def body(latents, conv_weight, gain, bias):
        _, frames, _, cols, ch = latents.shape
        group = GROUP
        all_frames = sections * frames
        rows = group * cols
        dma = pltpu.SemaphoreType.DMA
        vmem = pl.BlockSpec(memory_space=pltpu.VMEM)
        out = pl.pallas_call(
            functools.partial(kernel, sections, row_count, group),
            out_shape=jax.ShapeDtypeStruct((frames, cols, ch), jnp.bfloat16),
            in_specs=[pl.BlockSpec(memory_space=pl.ANY)] * 4,
            out_specs=vmem,
            scratch_shapes=[
                pltpu.VMEM((9 * ch, 3 * ch), jnp.bfloat16),
                pltpu.VMEM((3, all_frames + 2, cols, ch), jnp.bfloat16),
                pltpu.VMEM((all_frames, cols, ch), jnp.bfloat16),
                pltpu.VMEM((all_frames, cols, ch), jnp.bfloat16),
                pltpu.VMEM((rows, 3 * ch), jnp.float32),
                pltpu.VMEM((1, ch), jnp.float32),
                pltpu.VMEM((1, ch), jnp.float32),
                dma((3, 3, 3)),
                dma((3,)),
                dma((frames,)),
                dma((all_frames,)),
                dma((all_frames,)),
                dma((all_frames, 2)),
                dma((all_frames, 2)),
                dma((frames,)),
            ],
            compiler_params=pltpu.CompilerParams(
                collective_id=0, has_side_effects=True, vmem_limit_bytes=60 * 2**20
            ),
            cost_estimate=pl.CostEstimate(
                flops=2 * all_frames * cols * 27 * ch * ch,
                bytes_accessed=27 * ch * ch * 2,
                transcendentals=all_frames * cols * ch,
            ),
        )(latents.reshape(frames, cols, ch), conv_weight[0], gain, bias)
        return out.reshape(latents.shape)

    in_specs = (
        P("section", None, "rows", None, None),
        P("section", None, None, None, None, None),
        P("section", None),
        P("section", None),
    )
    out_specs = P("section", None, "rows", None, None)
    return jax.shard_map(body, mesh=mesh, in_specs=in_specs, out_specs=out_specs, check_vma=False)
```
